32 devices in a mesh: sector: 16 (over z, y, core), lift: 2 (over x).
Axes of the slice: x: 2, y: 2, z: 4, core: 2. Of those that a mesh axis runs over, the one named last changes fastest.
Arguments:
- right_side: float32 [128, 65536], P('lift', 'sector'), may hold values from -40 to 40
- diagonal: float32 [65536], P('sector'), may hold values from 1.9 to 2.6
- coupling: float32 [65536], P('sector'), may hold values from 0.3 to 0.94
- local_inverse: bfloat16 [64, 1024, 2048], P('sector'), may hold values from -0.1 to 0.6
- coarse_basis: bfloat16 [64, 16, 1024], P('sector'), may hold values from -0.1875 to 0.1875
- coarse_inverse: float32 [1024, 1024], P('sector', 'lift'), may hold values from -8 to 12
Outputs:
- solution: float32 [128, 65536], P('lift', 'sector')
- residual: float32 [128, 65536], P('lift', 'sector')
The draws below stay inside these ranges and needn't reach their ends.
All inputs are finite; a program needn't handle non-finite values.
Results may differ from the reference program's by a relative error of at most 0.019.
Values may be sent and summed in bfloat16 or wider, within the bound.
A program may use at most 128 MiB of HBM per device.

```python
import jax
import jax.numpy as jnp
from jax import lax

ORDER = 2048
OV = 512
MODES = 16
SWEEPS = 4
OUTER = 2
OWN = 1024
SUBS = 64
ROWS = 65536
NC = 1024
CASES = 128


def draw_right_side(key, part):
    keys = jax.random.split(key, 3)
    trend = jnp.exp(jnp.log(6.0) * (1.0 - jnp.arange(ROWS, dtype=jnp.float32) / ROWS)) / jnp.sqrt(6.0)
    rough = jnp.exp(jax.random.uniform(keys[1], (ROWS,), jnp.float32, jnp.log(0.5), jnp.log(2.0)))
    case_scale = jnp.exp(jax.random.uniform(keys[2], (CASES, 1), jnp.float32, jnp.log(0.2), jnp.log(2.0)))
    base = jnp.clip(jax.random.normal(keys[0], (CASES, ROWS), jnp.float32), -4.0, 4.0)
    return base * case_scale * trend[None, :] * rough[None, :]


def draw_local_inverse(key, part):
    keys = jax.random.split(key, 2)
    sigma = 0.1 / jnp.sqrt(float(ORDER))
    noise = jnp.clip(jax.random.normal(keys[0], (SUBS, OWN, ORDER), jnp.float32), -4.0, 4.0) * sigma
    level = 0.38 * jnp.exp(jax.random.uniform(keys[1], (SUBS, OWN, 1), jnp.float32, jnp.log(0.8), jnp.log(1.25)))
    placed = jnp.arange(ORDER)[None, None, :] == (jnp.arange(OWN) + OV)[None, :, None]
    return (noise + jnp.where(placed, level, 0.0)).astype(jnp.bfloat16)


def draw_coarse_inverse(key, part):
    keys = jax.random.split(key, 2)
    sigma = 1.0 / jnp.sqrt(float(NC))
    noise = jnp.clip(jax.random.normal(keys[0], (NC, NC), jnp.float32), -4.0, 4.0) * sigma
    level = jnp.exp(jax.random.uniform(keys[1], (NC,), jnp.float32, jnp.log(2.0), jnp.log(8.0)))
    return noise + jnp.diag(level)


def block_scale(key, shape, cuts, least, top_value):
    level = 1.0
    for axis_at, shards_of in cuts:
        steps = jax.random.uniform(jax.random.fold_in(jax.random.fold_in(key, 6), axis_at), (shards_of,), jnp.float32, least / len(cuts), top_value / len(cuts))
        level = level * jnp.repeat(jnp.exp(steps), shape[axis_at] // shards_of).reshape((-1,) + (1,) * (len(shape) - 1 - axis_at))
    return level


def normal_values(key, dims, deviation, bound, cuts=(), kind=jnp.bfloat16):
    drawn = jax.random.normal(key, dims, jnp.float32) * deviation
    if len(cuts) > 0:
        drawn = block_scale(key, dims, cuts, -0.22, 0.18) * drawn
    return jnp.clip(drawn, min=-bound, max=bound).astype(kind)


def setup_inputs(seed: int = 0) -> dict:
    key_list = jax.random.split(jax.random.key(seed), 7)
    return {
        "right_side": draw_right_side(jax.random.fold_in(key_list[6], 71), 0),
        "diagonal": jnp.clip(1.9 + 0.6999999 * jax.random.uniform(key_list[1], (ROWS,), jnp.float32) ** block_scale(key_list[1], (ROWS,), ((0, 16),), -0.2, 0.2), 1.9, 2.6),
        "coupling": jnp.clip(0.3 + 0.64 * jax.random.uniform(key_list[2], (ROWS,), jnp.float32) ** block_scale(key_list[2], (ROWS,), ((0, 16),), -0.2, 0.2), 0.3, 0.94),
        "local_inverse": draw_local_inverse(jax.random.fold_in(key_list[6], 71), 0),
        "coarse_basis": normal_values(key_list[4], (SUBS, MODES, OWN), OWN ** -0.5, 0.1875, ((0, 16),)),
        "coarse_inverse": draw_coarse_inverse(jax.random.fold_in(key_list[6], 71), 0),
    }


def apply_op(field, diagonal, coupling):
    return diagonal * field - coupling * (jnp.roll(field, 1, axis=1) + jnp.roll(field, -1, axis=1))


def reference(right_side, diagonal, coupling, local_inverse, coarse_basis, coarse_inverse):
    highest = lax.Precision.HIGHEST

    def correct(half_res):
        padded = jnp.concatenate([half_res[:, ROWS - OV:], half_res, half_res[:, :OV]], axis=1)

        def single(index):
            window = lax.dynamic_slice_in_dim(padded, index * OWN, ORDER, 1)
            inverse = lax.dynamic_index_in_dim(local_inverse, index, 0, keepdims=False)
            return jnp.dot(window.astype(jnp.float32), inverse.astype(jnp.float32).T, precision=highest)

        blocks = lax.map(single, jnp.arange(SUBS, dtype=jnp.int32))
        return jnp.transpose(blocks, (1, 0, 2)).reshape(CASES, ROWS)

    basis_wide = coarse_basis.astype(jnp.float32)
    solution = jnp.zeros_like(right_side)
    residual = right_side
    for outer_step in range(OUTER):
        update = correct(residual.astype(jnp.bfloat16))
        for sweep in range(SWEEPS - 1):
            sweep_res = (residual - apply_op(update, diagonal, coupling)).astype(jnp.bfloat16)
            update = update + correct(sweep_res)
        coarse_res = (residual - apply_op(update, diagonal, coupling)).astype(jnp.bfloat16)
        projected = jnp.einsum("cjk,jmk->cjm", coarse_res.reshape(CASES, SUBS, OWN).astype(jnp.float32), basis_wide, precision=highest).reshape(CASES, NC)
        coarse_sol = jnp.dot(projected, coarse_inverse.T, precision=highest)
        update = update + jnp.einsum("cjm,jmk->cjk", coarse_sol.reshape(CASES, SUBS, MODES), basis_wide, precision=highest).reshape(CASES, ROWS)
        image = apply_op(update, diagonal, coupling)
        alpha = jnp.sum(residual * image, axis=1) / (jnp.sum(image * image, axis=1) + 1e-6)
        solution = solution + alpha[:, None] * update
        residual = residual - alpha[:, None] * image
    return solution, residual
```

```python
import functools

import jax
import jax.numpy as jnp
from jax import lax
from jax.experimental import pallas as pl
from jax.experimental.pallas import tpu as pltpu
from jax.sharding import PartitionSpec as P

SWEEPS = 4
OUTER = 2
LANE = 128
F32 = jnp.float32
BF16 = jnp.bfloat16
NT = (((1,), (1,)), ((), ()))


def dot_nt(a, b):
    return lax.dot_general(a, b, NT, preferred_element_type=F32)


def kernel(
    ns, nl,
    rhs_ref, diag_ref, coup_ref, inv_ref, basis_ref, cinv_ref,
    sol_ref, res_ref,
    wv, u, img, h, snd, rcv, edge, esnd, ercv, bext, cx, gbuf, stat, sbuf,
    w_sem, hs_sem, hr_sem, es_sem, er_sem, ls_sem, lr_sem, ns_sem, nr_sem,
    gs_sem, gr_sem, ss_sem, sr_sem,
):
    cases, rows = rhs_ref.shape
    subs, own, order = inv_ref.shape
    margin = (order - own) // 2
    modes = basis_ref.shape[1]
    nm = subs * modes
    tile = wv.shape[1] // w_sem.shape[0]
    tiles = own // tile
    group = 16
    groups = cases // group
    cut = margin + 2 * LANE
    me = lax.axis_index("sector")
    lift = lax.axis_index("lift")
    right = lax.rem(me + 1, ns)
    left = lax.rem(me + ns - 1, ns)

    def w_copy(i):
        return pltpu.make_async_copy(
            inv_ref.at[:, pl.ds(i * tile, tile), :], wv.at[:, pl.ds(i * tile, tile), :], w_sem.at[i]
        )

    for i in range(tiles):
        w_copy(i).start()

    def remote(src, dst, send, recv, where):
        return pltpu.make_async_remote_copy(
            src_ref=src, dst_ref=dst, send_sem=send, recv_sem=recv,
            device_id=where, device_id_type=pl.DeviceIdType.MESH,
        )

    bext[...] = jnp.zeros_like(bext)
    for j in range(subs):
        bext[j * modes:(j + 1) * modes, LANE + j * own:LANE + (j + 1) * own] = basis_ref[j]
    cx[...] = jnp.zeros_like(cx)
    half = cinv_ref.shape[1]
    per = half // nm
    lanes = lax.broadcasted_iota(jnp.int32, (nm, LANE), 1)
    for d in range(per):
        start = d * nm
        base = (start // LANE) * LANE
        block = cinv_ref[:, base:base + LANE]
        if start > base:
            block = pltpu.roll(block, LANE - (start - base), 1)
        block = jnp.where(lanes < nm, block, 0.0).astype(BF16)
        cx[0:nm, pl.ds(pl.multiple_of((lift * per + d) * LANE, LANE), LANE)] = block
    res_ref[...] = rhs_ref[...]
    sol_ref[...] = jnp.zeros_like(sol_ref)

    barrier = pltpu.get_barrier_semaphore()

    def greet(k, carry):
        pl.semaphore_signal(
            barrier, inc=1, device_id={"sector": lax.rem(me + k, ns)},
            device_id_type=pl.DeviceIdType.MESH,
        )
        return carry

    lax.fori_loop(1, ns, greet, 0)
    for k in range(1, nl):
        pl.semaphore_signal(
            barrier, inc=1, device_id={"lift": lax.rem(lift + k, nl)},
            device_id_type=pl.DeviceIdType.MESH,
        )
    pl.semaphore_wait(barrier, ns - 1 + nl - 1)

    def lift_copy(k):
        part = cx.at[0:nm, pl.ds(pl.multiple_of(lift * per * LANE, LANE), per * LANE)]
        return remote(part, part, ls_sem.at[k], lr_sem.at[k], {"lift": lax.rem(lift + k, nl)})

    def lift_wait(k):
        source = lax.rem(lift + nl - k, nl)
        part = cx.at[0:nm, pl.ds(pl.multiple_of(source * per * LANE, LANE), per * LANE)]
        return remote(part, part, ls_sem.at[k], lr_sem.at[k], {"lift": lax.rem(lift + k, nl)})

    def neighbour_copies():
        return (
            remote(cx.at[nm - modes:nm], cx.at[nm:nm + modes], ns_sem.at[0], nr_sem.at[0], {"sector": right}),
            remote(cx.at[0:modes], cx.at[nm + modes:nm + 2 * modes], ns_sem.at[1], nr_sem.at[1], {"sector": left}),
            remote(
                basis_ref.at[subs - 1, :, own - LANE:own], bext.at[nm:nm + modes, 0:LANE],
                ns_sem.at[2], nr_sem.at[2], {"sector": right},
            ),
            remote(
                basis_ref.at[0, :, 0:LANE], bext.at[nm + modes:nm + 2 * modes, LANE + rows:2 * LANE + rows],
                ns_sem.at[3], nr_sem.at[3], {"sector": left},
            ),
        )

    for k in range(1, nl):
        lift_copy(k).start()

    lane_g = lax.broadcasted_iota(jnp.int32, (group, LANE), 1)
    lane_c = lax.broadcasted_iota(jnp.int32, (cases, LANE), 1)
    eye = lax.broadcasted_iota(jnp.int32, (cases, LANE), 0) == lane_c

    def pack(parts):
        out = jnp.zeros((parts[0].shape[0], LANE), F32)
        lane = lane_g
        for at, part in enumerate(parts):
            high = part.astype(BF16).astype(F32)
            out = jnp.where(lane == 2 * at, high, out)
            out = jnp.where(lane == 2 * at + 1, part - high, out)
        return out.astype(BF16)

    def applied(rs, c):
        x = u[rs, c * own:c * own + own + 2 * LANE]
        width = own + 2 * LANE
        both = pltpu.roll(x, 1, 1)[:, LANE:LANE + own] + pltpu.roll(x, width - 1, 1)[:, LANE:LANE + own]
        cols = slice(c * own, (c + 1) * own)
        return diag_ref[:, cols] * x[:, LANE:LANE + own] - coup_ref[:, cols] * both

    def halo_copies(t):
        return (
            remote(snd.at[0], rcv.at[t, 0], hs_sem.at[t, 0], hr_sem.at[t, 0], {"sector": left}),
            remote(snd.at[1], rcv.at[t, 1], hs_sem.at[t, 1], hr_sem.at[t, 1], {"sector": right}),
        )

    def rim_copies(o):
        return (
            remote(esnd.at[0], ercv.at[o, 0], es_sem.at[o, 0], er_sem.at[o, 0], {"sector": left}),
            remote(esnd.at[1], ercv.at[o, 1], es_sem.at[o, 1], er_sem.at[o, 1], {"sector": right}),
        )

    def gather_copy(o, k):
        return remote(
            gbuf.at[o, :, pl.ds(pl.multiple_of(me * LANE, LANE), LANE)],
            gbuf.at[o, :, pl.ds(pl.multiple_of(me * LANE, LANE), LANE)],
            gs_sem.at[o, k], gr_sem.at[o, k], {"sector": lax.rem(me + k, ns)},
        )

    def gather_wait(o, k):
        source = lax.rem(me + ns - k, ns)
        part = gbuf.at[o, :, pl.ds(pl.multiple_of(source * LANE, LANE), LANE)]
        return remote(part, part, gs_sem.at[o, k], gr_sem.at[o, k], {"sector": lax.rem(me + k, ns)})

    def sum_copy(o, k):
        return remote(
            sbuf.at[o, me], sbuf.at[o, me], ss_sem.at[o, k], sr_sem.at[o, k],
            {"sector": lax.rem(me + k, ns)},
        )

    def sum_wait(o, k):
        source = lax.rem(me + ns - k, ns)
        return remote(
            sbuf.at[o, source], sbuf.at[o, source], ss_sem.at[o, k], sr_sem.at[o, k],
            {"sector": lax.rem(me + k, ns)},
        )

    def sweep(t, carry):
        def residual_rows(g, carry):
            rs = pl.ds(pl.multiple_of(g * group, group), group)
            for c in range(subs):
                hf = res_ref[rs, c * own:(c + 1) * own] - applied(rs, c)
                hb = hf.astype(BF16)
                h[rs, c * own:(c + 1) * own] = hb
                if c == 0:
                    snd[0, rs, 0:margin] = hb[:, 0:margin]
                    edge[0, rs, :] = hf[:, 0:LANE]
                    snd[0, rs, margin:margin + LANE] = pack(
                        [u[rs, LANE:LANE + 1], hf[:, 0:1], jnp.broadcast_to(coup_ref[:, 0:1], (group, 1))]
                    )
                if c == subs - 1:
                    snd[1, rs, 0:margin] = hb[:, own - margin:own]
                    edge[1, rs, :] = hf[:, own - LANE:own]
                    snd[1, rs, margin:margin + LANE] = pack(
                        [
                            u[rs, LANE + rows - 1:LANE + rows], hf[:, own - 1:own],
                            jnp.broadcast_to(coup_ref[:, rows - 1:rows], (group, 1)),
                        ]
                    )
            return carry

        lax.fori_loop(0, groups, residual_rows, 0)
        to_left, to_right = halo_copies(t)
        to_left.start()
        to_right.start()

        def inner(i, carry):
            @pl.when(t == 0)
            def _():
                w_copy(i).wait()

            ws = pl.ds(pl.multiple_of(i * tile, tile), tile)
            for j in range(subs):
                low = cut if j == 0 else 0
                high = order - cut if j == subs - 1 else order
                shift = j * own - margin
                out = pl.ds(pl.multiple_of(LANE + j * own + i * tile, LANE), tile)
                u[:, out] += dot_nt(h[:, shift + low:shift + high], wv[j, ws, low:high])
            return carry

        lax.fori_loop(0, tiles, inner, 0, unroll=False)
        to_left.wait()
        to_right.wait()
        msg_high = rcv[t, 0, :, margin:margin + LANE].astype(F32)
        msg_low = rcv[t, 1, :, margin:margin + LANE].astype(F32)
        mine_low = snd[0, :, margin:margin + LANE].astype(F32)
        mine_high = snd[1, :, margin:margin + LANE].astype(F32)

        def part(msg, at):
            return msg[:, 2 * at:2 * at + 1] + msg[:, 2 * at + 1:2 * at + 2]

        tile_low = edge[0]
        h[:, 0:LANE] = jnp.where(
            lane_c == 0, tile_low + coup_ref[:, 0:LANE] * part(msg_low, 0), tile_low
        ).astype(BF16)
        tile_high = edge[1]
        h[:, rows - LANE:rows] = jnp.where(
            lane_c == LANE - 1, tile_high + coup_ref[:, rows - LANE:rows] * part(msg_high, 0), tile_high
        ).astype(BF16)
        halo_low = rcv[t, 1, :, margin - LANE:margin].astype(F32)
        rcv[t, 1, :, margin - LANE:margin] = jnp.where(
            lane_c == LANE - 1, part(msg_low, 1) + part(msg_low, 2) * part(mine_low, 0), halo_low
        ).astype(BF16)
        halo_high = rcv[t, 0, :, 0:LANE].astype(F32)
        rcv[t, 0, :, 0:LANE] = jnp.where(
            lane_c == 0, part(msg_high, 1) + part(msg_high, 2) * part(mine_high, 0), halo_high
        ).astype(BF16)

        def outer_part(i, carry):
            ws = pl.ds(pl.multiple_of(i * tile, tile), tile)
            out = pl.ds(pl.multiple_of(LANE + i * tile, LANE), tile)
            u[:, out] += dot_nt(rcv[t, 1, :, 0:margin], wv[0, ws, 0:margin]) + dot_nt(
                h[:, 0:cut - margin], wv[0, ws, margin:cut]
            )
            out = pl.ds(pl.multiple_of(LANE + (subs - 1) * own + i * tile, LANE), tile)
            u[:, out] += dot_nt(rcv[t, 0, :, 0:margin], wv[subs - 1, ws, order - margin:order]) + dot_nt(
                h[:, rows - (cut - margin):rows], wv[subs - 1, ws, order - cut:order - margin]
            )
            return carry

        lax.fori_loop(0, tiles, outer_part, 0, unroll=False)
        return carry

    def correction(o, carry):
        u[...] = jnp.zeros_like(u)
        lax.fori_loop(o * SWEEPS, (o + 1) * SWEEPS, sweep, 0, unroll=False)

        @pl.when(o == 0)
        def _():
            for k in range(1, nl):
                lift_wait(k).wait()
            for copy in neighbour_copies():
                copy.start()

        for g in range(groups):
            rs = slice(g * group, (g + 1) * group)
            esnd[0, rs, :] = pack([u[rs, LANE:LANE + 1]])
            esnd[1, rs, :] = pack([u[rs, LANE + rows - 1:LANE + rows]])
        to_left, to_right = rim_copies(o)
        to_left.start()
        to_right.start()
        to_left.wait()
        to_right.wait()
        msg = ercv[o, 1].astype(F32)
        u[:, 0:LANE] = jnp.broadcast_to(msg[:, 0:1] + msg[:, 1:2], (cases, LANE))
        msg = ercv[o, 0].astype(F32)
        u[:, LANE + rows:2 * LANE + rows] = jnp.broadcast_to(msg[:, 0:1] + msg[:, 1:2], (cases, LANE))

        def coarse_rows(g, carry):
            rs = pl.ds(pl.multiple_of(g * group, group), group)
            for c in range(subs):
                cols = slice(c * own, (c + 1) * own)
                h[rs, cols] = (res_ref[rs, cols] - applied(rs, c)).astype(BF16)
            return carry

        lax.fori_loop(0, groups, coarse_rows, 0)
        projected = dot_nt(h[...], bext[:, LANE:LANE + rows])
        gbuf[o, :, pl.ds(pl.multiple_of(me * LANE, LANE), LANE)] = projected.astype(BF16)

        def start_gather(k, carry):
            gather_copy(o, k).start()
            return carry

        lax.fori_loop(1, ns, start_gather, 0)

        def wait_gather(k, carry):
            gather_wait(o, k).wait()
            return carry

        lax.fori_loop(1, ns, wait_gather, 0)

        @pl.when(o == 0)
        def _():
            for copy in neighbour_copies():
                copy.wait()

        coarse = dot_nt(gbuf[o], cx[...]).astype(BF16)
        width = 2 * LANE + rows
        step = 2 * LANE
        for at in range(0, width, step):
            u[:, at:at + step] += jnp.dot(coarse, bext[:, at:at + step], preferred_element_type=F32)

        def image_rows(g, carry):
            rs = pl.ds(pl.multiple_of(g * group, group), group)
            first = jnp.zeros((group, LANE), F32)
            second = jnp.zeros((group, LANE), F32)
            for c in range(subs):
                cols = slice(c * own, (c + 1) * own)
                value = applied(rs, c)
                img[rs, cols] = value
                cross = res_ref[rs, cols] * value
                square = value * value
                for at in range(0, own, LANE):
                    first += cross[:, at:at + LANE]
                    second += square[:, at:at + LANE]
            stat[0, rs, :] = first
            stat[1, rs, :] = second
            return carry

        lax.fori_loop(0, groups, image_rows, 0)
        line = lax.broadcasted_iota(jnp.int32, (8, LANE), 0)
        row_sums = [
            jnp.sum(jnp.where(eye, jnp.sum(stat[at], axis=1, keepdims=True), 0.0), axis=0, keepdims=True)
            for at in range(2)
        ]
        sbuf[o, me] = jnp.where(line == 0, row_sums[0], jnp.where(line == 1, row_sums[1], 0.0))

        def start_sum(k, carry):
            sum_copy(o, k).start()
            return carry

        lax.fori_loop(1, ns, start_sum, 0)

        def wait_sum(k, carry):
            sum_wait(o, k).wait()
            return carry

        lax.fori_loop(1, ns, wait_sum, 0)
        totals = jnp.sum(sbuf[o], axis=0)
        alpha_row = totals[0:1] / (totals[1:2] + 1e-06)
        stat[0] = jnp.broadcast_to(
            jnp.sum(jnp.where(eye, alpha_row, 0.0), axis=1, keepdims=True), (cases, LANE)
        )

        def step_rows(g, carry):
            rs = pl.ds(pl.multiple_of(g * group, group), group)
            alpha = stat[0, rs, 0:1]
            for c in range(subs):
                cols = slice(c * own, (c + 1) * own)
                sol_ref[rs, cols] += alpha * u[rs, LANE + c * own:LANE + (c + 1) * own]
                res_ref[rs, cols] -= alpha * img[rs, cols]
            return carry

        lax.fori_loop(0, groups, step_rows, 0)
        return carry

    lax.fori_loop(0, OUTER, correction, 0, unroll=False)


def body(right_side, diagonal, coupling, local_inverse, coarse_basis, coarse_inverse):
    ns = lax.axis_size("sector")
    nl = lax.axis_size("lift")
    cases, rows = right_side.shape
    subs, own, order = local_inverse.shape
    modes = coarse_basis.shape[1]
    margin = (order - own) // 2
    steps = SWEEPS * OUTER
    tile = 256
    vmem = pl.BlockSpec(memory_space=pltpu.VMEM)
    dma = pltpu.SemaphoreType.DMA
    flops = 2 * cases * subs * own * order * steps
    return pl.pallas_call(
        functools.partial(kernel, ns, nl),
        out_shape=(
            jax.ShapeDtypeStruct((cases, rows), F32),
            jax.ShapeDtypeStruct((cases, rows), F32),
        ),
        in_specs=[vmem, vmem, vmem, pl.BlockSpec(memory_space=pl.ANY), vmem, vmem],
        out_specs=(vmem, vmem),
        scratch_shapes=[
            pltpu.VMEM((subs, own, order), BF16),
            pltpu.VMEM((cases, rows + 2 * LANE), F32),
            pltpu.VMEM((cases, rows), F32),
            pltpu.VMEM((cases, rows), BF16),
            pltpu.VMEM((2, cases, margin + LANE), BF16),
            pltpu.VMEM((steps, 2, cases, margin + LANE), BF16),
            pltpu.VMEM((2, cases, LANE), F32),
            pltpu.VMEM((2, cases, LANE), BF16),
            pltpu.VMEM((OUTER, 2, cases, LANE), BF16),
            pltpu.VMEM((LANE, rows + 2 * LANE), BF16),
            pltpu.VMEM((LANE, ns * LANE), BF16),
            pltpu.VMEM((OUTER, cases, ns * LANE), BF16),
            pltpu.VMEM((2, cases, LANE), F32),
            pltpu.VMEM((OUTER, ns, 8, LANE), F32),
            dma((own // tile,)),
            dma((steps, 2)), dma((steps, 2)),
            dma((OUTER, 2)), dma((OUTER, 2)),
            dma((nl,)), dma((nl,)),
            dma((4,)), dma((4,)),
            dma((OUTER, ns)), dma((OUTER, ns)),
            dma((OUTER, ns)), dma((OUTER, ns)),
        ],
        compiler_params=pltpu.CompilerParams(
            collective_id=0, has_side_effects=True, vmem_limit_bytes=56 * 1024 * 1024
        ),
        cost_estimate=pl.CostEstimate(
            flops=flops, bytes_accessed=2 * subs * own * order, transcendentals=0
        ),
    )(right_side, diagonal[None, :], coupling[None, :], local_inverse, coarse_basis, coarse_inverse)


def solution(mesh):
    in_specs = (
        P("lift", "sector"),
        P("sector"),
        P("sector"),
        P("sector", None, None),
        P("sector", None, None),
        P("sector", "lift"),
    )
    out_specs = (P("lift", "sector"), P("lift", "sector"))
    return jax.shard_map(body, mesh=mesh, in_specs=in_specs, out_specs=out_specs, check_vma=False)
```

```python
import functools

import jax
import jax.numpy as jnp
from jax import lax
from jax.experimental import pallas as pl
from jax.experimental.pallas import tpu as pltpu
from jax.sharding import PartitionSpec as P

SWEEPS = 4
OUTER = 2
LANE = 128
F32 = jnp.float32
BF16 = jnp.bfloat16
NT = (((1,), (1,)), ((), ()))


def dot_nt(a, b):
    return lax.dot_general(a, b, NT, preferred_element_type=F32)


def times(field, inverse):
    return dot_nt(inverse, field)


def kernel(
    ns, nl,
    rhs_ref, diag_ref, coup_ref, inv_ref, basis_ref, cinv_ref,
    sol_ref, res_ref, last_ref, img, alpha_ref,
    wv, u, h, snd, rcv, edge, esnd, ercv, bext, cx, gbuf, stat, sbuf,
    w_sem, hs_sem, hr_sem, es_sem, er_sem, ls_sem, lr_sem, ns_sem, nr_sem,
    gs_sem, gr_sem, ss_sem, sr_sem,
):
    cases, rows = rhs_ref.shape
    subs, own, order = inv_ref.shape
    margin = (order - own) // 2
    modes = basis_ref.shape[1]
    nm = subs * modes
    tile = wv.shape[1] // w_sem.shape[0]
    tiles = own // tile
    group = 16
    groups = cases // group
    cut = margin + 2 * LANE
    me = lax.axis_index("sector")
    lift = lax.axis_index("lift")
    right = lax.rem(me + 1, ns)
    left = lax.rem(me + ns - 1, ns)

    def w_copy(i):
        return pltpu.make_async_copy(
            inv_ref.at[:, pl.ds(i * tile, tile), :], wv.at[:, pl.ds(i * tile, tile), :], w_sem.at[i]
        )

    for i in range(tiles):
        w_copy(i).start()

    def remote(src, dst, send, recv, where):
        return pltpu.make_async_remote_copy(
            src_ref=src, dst_ref=dst, send_sem=send, recv_sem=recv,
            device_id=where, device_id_type=pl.DeviceIdType.MESH,
        )

    bext[...] = jnp.zeros_like(bext)
    for j in range(subs):
        bext[j * modes:(j + 1) * modes, LANE + j * own:LANE + (j + 1) * own] = basis_ref[j]
    cx[...] = jnp.zeros_like(cx)
    half = cinv_ref.shape[1]
    per = half // nm
    lanes = lax.broadcasted_iota(jnp.int32, (nm, LANE), 1)
    for d in range(per):
        start = d * nm
        base = (start // LANE) * LANE
        block = cinv_ref[:, base:base + LANE]
        if start > base:
            block = pltpu.roll(block, LANE - (start - base), 1)
        block = jnp.where(lanes < nm, block, 0.0).astype(BF16)
        cx[0:nm, pl.ds(pl.multiple_of((lift * per + d) * LANE, LANE), LANE)] = block
    res_ref[...] = rhs_ref[...]
    sol_ref[...] = jnp.zeros_like(sol_ref)

    barrier = pltpu.get_barrier_semaphore()

    def greet(k, carry):
        pl.semaphore_signal(
            barrier, inc=1, device_id={"sector": lax.rem(me + k, ns)},
            device_id_type=pl.DeviceIdType.MESH,
        )
        return carry

    lax.fori_loop(1, ns, greet, 0)
    for k in range(1, nl):
        pl.semaphore_signal(
            barrier, inc=1, device_id={"lift": lax.rem(lift + k, nl)},
            device_id_type=pl.DeviceIdType.MESH,
        )
    pl.semaphore_wait(barrier, ns - 1 + nl - 1)

    def lift_copy(k):
        part = cx.at[0:nm, pl.ds(pl.multiple_of(lift * per * LANE, LANE), per * LANE)]
        return remote(part, part, ls_sem.at[k], lr_sem.at[k], {"lift": lax.rem(lift + k, nl)})

    def lift_wait(k):
        source = lax.rem(lift + nl - k, nl)
        part = cx.at[0:nm, pl.ds(pl.multiple_of(source * per * LANE, LANE), per * LANE)]
        return remote(part, part, ls_sem.at[k], lr_sem.at[k], {"lift": lax.rem(lift + k, nl)})

    def neighbour_copies():
        return (
            remote(cx.at[nm - modes:nm], cx.at[nm:nm + modes], ns_sem.at[0], nr_sem.at[0], {"sector": right}),
            remote(cx.at[0:modes], cx.at[nm + modes:nm + 2 * modes], ns_sem.at[1], nr_sem.at[1], {"sector": left}),
            remote(
                basis_ref.at[subs - 1, :, own - LANE:own], bext.at[nm:nm + modes, 0:LANE],
                ns_sem.at[2], nr_sem.at[2], {"sector": right},
            ),
            remote(
                basis_ref.at[0, :, 0:LANE], bext.at[nm + modes:nm + 2 * modes, LANE + rows:2 * LANE + rows],
                ns_sem.at[3], nr_sem.at[3], {"sector": left},
            ),
        )

    for k in range(1, nl):
        lift_copy(k).start()

    lane_g = lax.broadcasted_iota(jnp.int32, (group, LANE), 1)
    lane_c = lax.broadcasted_iota(jnp.int32, (cases, LANE), 1)
    eye = lax.broadcasted_iota(jnp.int32, (cases, LANE), 0) == lane_c

    def pack(parts):
        out = jnp.zeros((parts[0].shape[0], LANE), F32)
        lane = lane_g
        for at, part in enumerate(parts):
            high = part.astype(BF16).astype(F32)
            out = jnp.where(lane == 2 * at, high, out)
            out = jnp.where(lane == 2 * at + 1, part - high, out)
        return out.astype(BF16)

    def applied(rs, c):
        x = u[rs, c * own:c * own + own + 2 * LANE]
        width = own + 2 * LANE
        both = pltpu.roll(x, 1, 1)[:, LANE:LANE + own] + pltpu.roll(x, width - 1, 1)[:, LANE:LANE + own]
        cols = slice(c * own, (c + 1) * own)
        return diag_ref[:, cols] * x[:, LANE:LANE + own] - coup_ref[:, cols] * both

    def halo_copies(t):
        return (
            remote(snd.at[0], rcv.at[t, 0], hs_sem.at[t, 0], hr_sem.at[t, 0], {"sector": left}),
            remote(snd.at[1], rcv.at[t, 1], hs_sem.at[t, 1], hr_sem.at[t, 1], {"sector": right}),
        )

    def rim_copies(o):
        return (
            remote(esnd.at[0], ercv.at[o, 0], es_sem.at[o, 0], er_sem.at[o, 0], {"sector": left}),
            remote(esnd.at[1], ercv.at[o, 1], es_sem.at[o, 1], er_sem.at[o, 1], {"sector": right}),
        )

    def gather_copy(o, k):
        return remote(
            gbuf.at[o, :, pl.ds(pl.multiple_of(me * LANE, LANE), LANE)],
            gbuf.at[o, :, pl.ds(pl.multiple_of(me * LANE, LANE), LANE)],
            gs_sem.at[o, k], gr_sem.at[o, k], {"sector": lax.rem(me + k, ns)},
        )

    def gather_wait(o, k):
        source = lax.rem(me + ns - k, ns)
        part = gbuf.at[o, :, pl.ds(pl.multiple_of(source * LANE, LANE), LANE)]
        return remote(part, part, gs_sem.at[o, k], gr_sem.at[o, k], {"sector": lax.rem(me + k, ns)})

    def sum_copy(o, k):
        return remote(
            sbuf.at[o, me], sbuf.at[o, me], ss_sem.at[o, k], sr_sem.at[o, k],
            {"sector": lax.rem(me + k, ns)},
        )

    def sum_wait(o, k):
        source = lax.rem(me + ns - k, ns)
        return remote(
            sbuf.at[o, source], sbuf.at[o, source], ss_sem.at[o, k], sr_sem.at[o, k],
            {"sector": lax.rem(me + k, ns)},
        )

    def sweep(t, carry):
        def residual_rows(g, carry):
            rs = pl.ds(pl.multiple_of(g * group, group), group)
            for c in range(subs):
                hf = res_ref[rs, c * own:(c + 1) * own] - applied(rs, c)
                hb = hf.astype(BF16)
                h[rs, c * own:(c + 1) * own] = hb
                if c == 0:
                    snd[0, rs, 0:margin] = hb[:, 0:margin]
                    edge[0, rs, :] = hf[:, 0:LANE]
                    snd[0, rs, margin:margin + LANE] = pack(
                        [u[rs, LANE:LANE + 1], hf[:, 0:1], jnp.broadcast_to(coup_ref[:, 0:1], (group, 1))]
                    )
                if c == subs - 1:
                    snd[1, rs, 0:margin] = hb[:, own - margin:own]
                    edge[1, rs, :] = hf[:, own - LANE:own]
                    snd[1, rs, margin:margin + LANE] = pack(
                        [
                            u[rs, LANE + rows - 1:LANE + rows], hf[:, own - 1:own],
                            jnp.broadcast_to(coup_ref[:, rows - 1:rows], (group, 1)),
                        ]
                    )
            return carry

        lax.fori_loop(0, groups, residual_rows, 0)
        to_left, to_right = halo_copies(t)
        to_left.start()
        to_right.start()

        def inner(i, carry):
            @pl.when(t == 0)
            def _():
                w_copy(i).wait()

            ws = pl.ds(pl.multiple_of(i * tile, tile), tile)
            for j in range(subs):
                low = cut if j == 0 else 0
                high = order - cut if j == subs - 1 else order
                shift = j * own - margin
                out = pl.ds(pl.multiple_of(LANE + j * own + i * tile, LANE), tile)
                u[:, out] += times(h[:, shift + low:shift + high], wv[j, ws, low:high]).T
            return carry

        lax.fori_loop(0, tiles, inner, 0, unroll=False)
        to_left.wait()
        to_right.wait()
        msg_high = rcv[t, 0, :, margin:margin + LANE].astype(F32)
        msg_low = rcv[t, 1, :, margin:margin + LANE].astype(F32)
        mine_low = snd[0, :, margin:margin + LANE].astype(F32)
        mine_high = snd[1, :, margin:margin + LANE].astype(F32)

        def part(msg, at):
            return msg[:, 2 * at:2 * at + 1] + msg[:, 2 * at + 1:2 * at + 2]

        tile_low = edge[0]
        h[:, 0:LANE] = jnp.where(
            lane_c == 0, tile_low + coup_ref[:, 0:LANE] * part(msg_low, 0), tile_low
        ).astype(BF16)
        tile_high = edge[1]
        h[:, rows - LANE:rows] = jnp.where(
            lane_c == LANE - 1, tile_high + coup_ref[:, rows - LANE:rows] * part(msg_high, 0), tile_high
        ).astype(BF16)
        halo_low = rcv[t, 1, :, margin - LANE:margin].astype(F32)
        rcv[t, 1, :, margin - LANE:margin] = jnp.where(
            lane_c == LANE - 1, part(msg_low, 1) + part(msg_low, 2) * part(mine_low, 0), halo_low
        ).astype(BF16)
        halo_high = rcv[t, 0, :, 0:LANE].astype(F32)
        rcv[t, 0, :, 0:LANE] = jnp.where(
            lane_c == 0, part(msg_high, 1) + part(msg_high, 2) * part(mine_high, 0), halo_high
        ).astype(BF16)

        def outer_part(i, carry):
            ws = pl.ds(pl.multiple_of(i * tile, tile), tile)
            out = pl.ds(pl.multiple_of(LANE + i * tile, LANE), tile)
            u[:, out] += (
                times(rcv[t, 1, :, 0:margin], wv[0, ws, 0:margin])
                + times(h[:, 0:cut - margin], wv[0, ws, margin:cut])
            ).T
            out = pl.ds(pl.multiple_of(LANE + (subs - 1) * own + i * tile, LANE), tile)
            u[:, out] += (
                times(rcv[t, 0, :, 0:margin], wv[subs - 1, ws, order - margin:order])
                + times(h[:, rows - (cut - margin):rows], wv[subs - 1, ws, order - cut:order - margin])
            ).T
            return carry

        lax.fori_loop(0, tiles, outer_part, 0, unroll=False)
        return carry

    def correction(o, carry):
        u[...] = jnp.zeros_like(u)
        lax.fori_loop(o * SWEEPS, (o + 1) * SWEEPS, sweep, 0, unroll=False)

        @pl.when(o == 0)
        def _():
            for k in range(1, nl):
                lift_wait(k).wait()
            for copy in neighbour_copies():
                copy.start()

        for g in range(groups):
            rs = slice(g * group, (g + 1) * group)
            esnd[0, rs, :] = pack([u[rs, LANE:LANE + 1]])
            esnd[1, rs, :] = pack([u[rs, LANE + rows - 1:LANE + rows]])
        to_left, to_right = rim_copies(o)
        to_left.start()
        to_right.start()
        to_left.wait()
        to_right.wait()
        msg = ercv[o, 1].astype(F32)
        u[:, 0:LANE] = jnp.broadcast_to(msg[:, 0:1] + msg[:, 1:2], (cases, LANE))
        msg = ercv[o, 0].astype(F32)
        u[:, LANE + rows:2 * LANE + rows] = jnp.broadcast_to(msg[:, 0:1] + msg[:, 1:2], (cases, LANE))

        def coarse_rows(g, carry):
            rs = pl.ds(pl.multiple_of(g * group, group), group)
            for c in range(subs):
                cols = slice(c * own, (c + 1) * own)
                h[rs, cols] = (res_ref[rs, cols] - applied(rs, c)).astype(BF16)
            return carry

        lax.fori_loop(0, groups, coarse_rows, 0)
        projected = dot_nt(h[...], bext[:, LANE:LANE + rows])
        gbuf[o, :, pl.ds(pl.multiple_of(me * LANE, LANE), LANE)] = projected.astype(BF16)

        def start_gather(k, carry):
            gather_copy(o, k).start()
            return carry

        lax.fori_loop(1, ns, start_gather, 0)

        def wait_gather(k, carry):
            gather_wait(o, k).wait()
            return carry

        lax.fori_loop(1, ns, wait_gather, 0)

        @pl.when(o == 0)
        def _():
            for copy in neighbour_copies():
                copy.wait()

        coarse = dot_nt(gbuf[o], cx[...]).astype(BF16)
        width = 2 * LANE + rows
        step = 2 * LANE
        for at in range(0, width, step):
            u[:, at:at + step] += jnp.dot(coarse, bext[:, at:at + step], preferred_element_type=F32)

        def image_rows(g, carry):
            rs = pl.ds(pl.multiple_of(g * group, group), group)
            first = jnp.zeros((group, LANE), F32)
            second = jnp.zeros((group, LANE), F32)
            for c in range(subs):
                cols = slice(c * own, (c + 1) * own)
                value = applied(rs, c)
                img[rs, cols] = value
                cross = res_ref[rs, cols] * value
                square = value * value
                for at in range(0, own, LANE):
                    first += cross[:, at:at + LANE]
                    second += square[:, at:at + LANE]
            stat[0, rs, :] = first
            stat[1, rs, :] = second
            return carry

        lax.fori_loop(0, groups, image_rows, 0)
        line = lax.broadcasted_iota(jnp.int32, (8, LANE), 0)
        row_sums = [
            jnp.sum(jnp.where(eye, jnp.sum(stat[at], axis=1, keepdims=True), 0.0), axis=0, keepdims=True)
            for at in range(2)
        ]
        sbuf[o, me] = jnp.where(line == 0, row_sums[0], jnp.where(line == 1, row_sums[1], 0.0))

        def start_sum(k, carry):
            sum_copy(o, k).start()
            return carry

        lax.fori_loop(1, ns, start_sum, 0)

        def wait_sum(k, carry):
            sum_wait(o, k).wait()
            return carry

        lax.fori_loop(1, ns, wait_sum, 0)
        totals = jnp.sum(sbuf[o], axis=0)
        alpha_row = totals[0:1] / (totals[1:2] + 1e-06)
        alpha_ref[...] = jnp.broadcast_to(
            jnp.sum(jnp.where(eye, alpha_row, 0.0), axis=1, keepdims=True), (cases, LANE)
        )

        def step_rows(g, carry):
            rs = pl.ds(pl.multiple_of(g * group, group), group)
            alpha = alpha_ref[rs, 0:1]
            for c in range(subs):
                cols = slice(c * own, (c + 1) * own)
                sol_ref[rs, cols] += alpha * u[rs, LANE + c * own:LANE + (c + 1) * own]
                res_ref[rs, cols] -= alpha * img[rs, cols]
            return carry

        @pl.when(o < OUTER - 1)
        def _():
            lax.fori_loop(0, groups, step_rows, 0)

        return carry

    lax.fori_loop(0, OUTER, correction, 0, unroll=False)
    last_ref[...] = u[:, LANE:LANE + rows]


def body(right_side, diagonal, coupling, local_inverse, coarse_basis, coarse_inverse):
    ns = lax.axis_size("sector")
    nl = lax.axis_size("lift")
    cases, rows = right_side.shape
    subs, own, order = local_inverse.shape
    modes = coarse_basis.shape[1]
    margin = (order - own) // 2
    steps = SWEEPS * OUTER
    tile = 256
    vmem = pl.BlockSpec(memory_space=pltpu.VMEM)
    dma = pltpu.SemaphoreType.DMA
    flops = 2 * cases * subs * own * order * steps
    solved, residual, update, image, alpha = pl.pallas_call(
        functools.partial(kernel, ns, nl),
        out_shape=(jax.ShapeDtypeStruct((cases, rows), F32),) * 4
        + (jax.ShapeDtypeStruct((cases, LANE), F32),),
        in_specs=[vmem, vmem, vmem, pl.BlockSpec(memory_space=pl.ANY), vmem, vmem],
        out_specs=(vmem,) * 5,
        scratch_shapes=[
            pltpu.VMEM((subs, own, order), BF16),
            pltpu.VMEM((cases, rows + 2 * LANE), F32),
            pltpu.VMEM((cases, rows), BF16),
            pltpu.VMEM((2, cases, margin + LANE), BF16),
            pltpu.VMEM((steps, 2, cases, margin + LANE), BF16),
            pltpu.VMEM((2, cases, LANE), F32),
            pltpu.VMEM((2, cases, LANE), BF16),
            pltpu.VMEM((OUTER, 2, cases, LANE), BF16),
            pltpu.VMEM((LANE, rows + 2 * LANE), BF16),
            pltpu.VMEM((LANE, ns * LANE), BF16),
            pltpu.VMEM((OUTER, cases, ns * LANE), BF16),
            pltpu.VMEM((2, cases, LANE), F32),
            pltpu.VMEM((OUTER, ns, 8, LANE), F32),
            dma((own // tile,)),
            dma((steps, 2)), dma((steps, 2)),
            dma((OUTER, 2)), dma((OUTER, 2)),
            dma((nl,)), dma((nl,)),
            dma((4,)), dma((4,)),
            dma((OUTER, ns)), dma((OUTER, ns)),
            dma((OUTER, ns)), dma((OUTER, ns)),
        ],
        compiler_params=pltpu.CompilerParams(
            collective_id=0, has_side_effects=True, vmem_limit_bytes=56 * 1024 * 1024
        ),
        cost_estimate=pl.CostEstimate(
            flops=flops, bytes_accessed=2 * subs * own * order, transcendentals=0
        ),
    )(right_side, diagonal[None, :], coupling[None, :], local_inverse, coarse_basis, coarse_inverse)
    alpha = alpha[:, 0:1]
    return solved + alpha * update, residual - alpha * image


def solution(mesh):
    in_specs = (
        P("lift", "sector"),
        P("sector"),
        P("sector"),
        P("sector", None, None),
        P("sector", None, None),
        P("sector", "lift"),
    )
    out_specs = (P("lift", "sector"), P("lift", "sector"))
    return jax.shard_map(body, mesh=mesh, in_specs=in_specs, out_specs=out_specs, check_vma=False)
```

```python
import functools

import jax
import jax.numpy as jnp
from jax import lax
from jax.experimental import pallas as pl
from jax.experimental.pallas import tpu as pltpu
from jax.sharding import PartitionSpec as P

SWEEPS = 4
OUTER = 2
LANE = 128
F32 = jnp.float32
BF16 = jnp.bfloat16
NT = (((1,), (1,)), ((), ()))


def dot_nt(a, b):
    return lax.dot_general(a, b, NT, preferred_element_type=F32)


def times(field, inverse):
    return dot_nt(inverse, field)


def kernel(
    ns, nl,
    rhs_ref, diag_ref, coup_ref, inv_ref, basis_ref, cinv_ref,
    sol_out, res_out, last_out, img_out, alpha_ref,
    wv, u, keep, first, sol, field, h, snd, rcv, edge, esnd, ercv, bext, cx, cy, gbuf, stat, sbuf,
    r_sem, o_sem, w_sem, hs_sem, hr_sem, es_sem, er_sem, ls_sem, lr_sem, ns_sem, nr_sem,
    gs_sem, gr_sem, ss_sem, sr_sem,
):
    cases, rows = rhs_ref.shape
    subs, own, order = inv_ref.shape
    margin = (order - own) // 2
    modes = basis_ref.shape[1]
    nm = subs * modes
    tile = wv.shape[1] // w_sem.shape[0]
    tiles = own // tile
    group = 16
    groups = cases // group
    cut = margin + 2 * LANE
    me = lax.axis_index("sector")
    lift = lax.axis_index("lift")
    right = lax.rem(me + 1, ns)
    left = lax.rem(me + ns - 1, ns)

    def w_copy(i):
        return pltpu.make_async_copy(
            inv_ref.at[:, pl.ds(i * tile, tile), :], wv.at[:, pl.ds(i * tile, tile), :], w_sem.at[i]
        )

    rhs_copy = pltpu.make_async_copy(rhs_ref, field.at[0], r_sem)
    rhs_copy.start()
    for i in range(tiles):
        w_copy(i).start()
    result_copies = (
        pltpu.make_async_copy(sol, sol_out, o_sem.at[0]),
        pltpu.make_async_copy(field.at[0], res_out, o_sem.at[1]),
        pltpu.make_async_copy(u.at[:, LANE:LANE + rows], last_out, o_sem.at[2]),
        pltpu.make_async_copy(field.at[1], img_out, o_sem.at[3]),
    )

    def remote(src, dst, send, recv, where):
        return pltpu.make_async_remote_copy(
            src_ref=src, dst_ref=dst, send_sem=send, recv_sem=recv,
            device_id=where, device_id_type=pl.DeviceIdType.MESH,
        )

    bext[...] = jnp.zeros_like(bext)
    for j in range(subs):
        bext[j * modes:(j + 1) * modes, LANE + j * own:LANE + (j + 1) * own] = basis_ref[j]
    cx[...] = jnp.zeros_like(cx)
    half = cinv_ref.shape[1]
    per = half // nm
    lanes = lax.broadcasted_iota(jnp.int32, (nm, LANE), 1)
    for d in range(per):
        start = d * nm
        base = (start // LANE) * LANE
        block = cinv_ref[:, base:base + LANE]
        if start > base:
            block = pltpu.roll(block, LANE - (start - base), 1)
        block = jnp.where(lanes < nm, block, 0.0).astype(BF16)
        cx[0:nm, pl.ds(pl.multiple_of((lift * per + d) * LANE, LANE), LANE)] = block
    barrier = pltpu.get_barrier_semaphore()

    def greet(k, carry):
        pl.semaphore_signal(
            barrier, inc=1, device_id={"sector": lax.rem(me + k, ns)},
            device_id_type=pl.DeviceIdType.MESH,
        )
        return carry

    lax.fori_loop(1, ns, greet, 0)
    for k in range(1, nl):
        pl.semaphore_signal(
            barrier, inc=1, device_id={"lift": lax.rem(lift + k, nl)},
            device_id_type=pl.DeviceIdType.MESH,
        )
    h[...] = jnp.zeros_like(h)
    u[...] = jnp.zeros_like(u)
    sol[...] = jnp.zeros_like(sol)
    pl.semaphore_wait(barrier, ns - 1 + nl - 1)

    def lift_copy(k):
        part = cx.at[0:nm, pl.ds(pl.multiple_of(lift * per * LANE, LANE), per * LANE)]
        return remote(part, part, ls_sem.at[k], lr_sem.at[k], {"lift": lax.rem(lift + k, nl)})

    def lift_wait(k):
        source = lax.rem(lift + nl - k, nl)
        part = cx.at[0:nm, pl.ds(pl.multiple_of(source * per * LANE, LANE), per * LANE)]
        return remote(part, part, ls_sem.at[k], lr_sem.at[k], {"lift": lax.rem(lift + k, nl)})

    def neighbour_copies():
        return (
            remote(cx.at[nm - modes:nm], cx.at[nm:nm + modes], ns_sem.at[0], nr_sem.at[0], {"sector": right}),
            remote(cx.at[0:modes], cx.at[nm + modes:nm + 2 * modes], ns_sem.at[1], nr_sem.at[1], {"sector": left}),
            remote(
                basis_ref.at[subs - 1, :, own - LANE:own], bext.at[nm:nm + modes, 0:LANE],
                ns_sem.at[2], nr_sem.at[2], {"sector": right},
            ),
            remote(
                basis_ref.at[0, :, 0:LANE], bext.at[nm + modes:nm + 2 * modes, LANE + rows:2 * LANE + rows],
                ns_sem.at[3], nr_sem.at[3], {"sector": left},
            ),
        )

    for k in range(1, nl):
        lift_copy(k).start()

    lane_g = lax.broadcasted_iota(jnp.int32, (group, LANE), 1)
    lane_c = lax.broadcasted_iota(jnp.int32, (cases, LANE), 1)
    eye = lax.broadcasted_iota(jnp.int32, (cases, LANE), 0) == lane_c

    def pack(parts):
        out = jnp.zeros((parts[0].shape[0], LANE), F32)
        lane = lane_g
        for at, part in enumerate(parts):
            high = part.astype(BF16).astype(F32)
            out = jnp.where(lane == 2 * at, high, out)
            out = jnp.where(lane == 2 * at + 1, part - high, out)
        return out.astype(BF16)

    def applied(rs, at, width):
        x = u[rs, at:at + width + 2 * LANE]
        span = width + 2 * LANE
        both = pltpu.roll(x, 1, 1)[:, LANE:LANE + width] + pltpu.roll(x, span - 1, 1)[:, LANE:LANE + width]
        cols = slice(at, at + width)
        return diag_ref[:, cols] * x[:, LANE:LANE + width] - coup_ref[:, cols] * both

    def part(msg, at):
        return msg[:, 2 * at:2 * at + 1] + msg[:, 2 * at + 1:2 * at + 2]

    def halo_copies(t):
        return (
            remote(snd.at[0], rcv.at[t, 0], hs_sem.at[t, 0], hr_sem.at[t, 0], {"sector": right}),
            remote(snd.at[1], rcv.at[t, 1], hs_sem.at[t, 1], hr_sem.at[t, 1], {"sector": left}),
        )

    def rim_copies(o):
        return (
            remote(esnd.at[0], ercv.at[o, 0], es_sem.at[o, 0], er_sem.at[o, 0], {"sector": right}),
            remote(esnd.at[1], ercv.at[o, 1], es_sem.at[o, 1], er_sem.at[o, 1], {"sector": left}),
        )

    def gather_copy(o, k):
        return remote(
            gbuf.at[o, :, pl.ds(pl.multiple_of(me * LANE, LANE), LANE)],
            gbuf.at[o, :, pl.ds(pl.multiple_of(me * LANE, LANE), LANE)],
            gs_sem.at[o, k], gr_sem.at[o, k], {"sector": lax.rem(me + k, ns)},
        )

    def gather_wait(o, k):
        source = lax.rem(me + ns - k, ns)
        part = gbuf.at[o, :, pl.ds(pl.multiple_of(source * LANE, LANE), LANE)]
        return remote(part, part, gs_sem.at[o, k], gr_sem.at[o, k], {"sector": lax.rem(me + k, ns)})

    def sum_copy(o, k):
        return remote(
            sbuf.at[o, me], sbuf.at[o, me], ss_sem.at[o, k], sr_sem.at[o, k],
            {"sector": lax.rem(me + k, ns)},
        )

    def sum_wait(o, k):
        source = lax.rem(me + ns - k, ns)
        return remote(
            sbuf.at[o, source], sbuf.at[o, source], ss_sem.at[o, k], sr_sem.at[o, k],
            {"sector": lax.rem(me + k, ns)},
        )

    def sweep(t, src):
        def low_rows(g, carry):
            rs = pl.ds(pl.multiple_of(g * group, group), group)
            hf = field[src, rs, 0:margin] - applied(rs, 0, margin)
            hb = hf.astype(BF16)
            h[rs, LANE:LANE + margin] = hb
            snd[1, rs, 0:margin] = hb
            edge[0, rs, :] = hf[:, 0:LANE]
            snd[1, rs, margin:margin + LANE] = pack(
                [u[rs, LANE:LANE + 1], hf[:, 0:1], jnp.broadcast_to(coup_ref[:, 0:1], (group, 1))]
            )
            hf = field[src, rs, rows - margin:rows] - applied(rs, rows - margin, margin)
            hb = hf.astype(BF16)
            h[rs, LANE + rows - margin:LANE + rows] = hb
            snd[0, rs, 0:margin] = hb
            edge[1, rs, :] = hf[:, margin - LANE:margin]
            snd[0, rs, margin:margin + LANE] = pack(
                [
                    u[rs, LANE + rows - 1:LANE + rows], hf[:, margin - 1:margin],
                    jnp.broadcast_to(coup_ref[:, rows - 1:rows], (group, 1)),
                ]
            )
            return carry

        lax.fori_loop(0, groups, low_rows, 0, unroll=True)
        copies = halo_copies(t)
        for copy in copies:
            copy.start()

        def middle_rows(g, carry):
            rs = pl.ds(pl.multiple_of(g * group, group), group)
            for at in range(margin, rows - margin, own):
                width = min(own, rows - margin - at)
                hf = field[src, rs, at:at + width] - applied(rs, at, width)
                h[rs, LANE + at:LANE + at + width] = hf.astype(BF16)
            return carry

        lax.fori_loop(0, groups, middle_rows, 0)

        @pl.when(t == 0)
        def _():
            for k in range(1, nl):
                lift_wait(k).wait()
            for copy in neighbour_copies():
                copy.start()
            for i in range(tiles):
                w_copy(i).wait()

        def inner(i, carry):
            ws = pl.ds(pl.multiple_of(i * tile, tile), tile)
            for j in range(subs):
                low = cut if j == 0 else 0
                high = order - cut if j == subs - 1 else order
                shift = LANE + j * own - margin
                out = pl.ds(pl.multiple_of(LANE + j * own + i * tile, LANE), tile)
                u[:, out] += times(h[:, shift + low:shift + high], wv[j, ws, low:high]).T
            return carry

        lax.fori_loop(0, tiles, inner, 0, unroll=True)
        for copy in copies:
            copy.wait()
        msg_low = rcv[t, 0, :, margin:margin + LANE].astype(F32)
        msg_high = rcv[t, 1, :, margin:margin + LANE].astype(F32)
        mine_low = snd[1, :, margin:margin + LANE].astype(F32)
        mine_high = snd[0, :, margin:margin + LANE].astype(F32)
        tile_low = edge[0]
        h[:, LANE:2 * LANE] = jnp.where(
            lane_c == 0, tile_low + coup_ref[:, 0:LANE] * part(msg_low, 0), tile_low
        ).astype(BF16)
        tile_high = edge[1]
        h[:, rows:LANE + rows] = jnp.where(
            lane_c == LANE - 1, tile_high + coup_ref[:, rows - LANE:rows] * part(msg_high, 0), tile_high
        ).astype(BF16)
        halo_low = rcv[t, 0, :, margin - LANE:margin].astype(F32)
        rcv[t, 0, :, margin - LANE:margin] = jnp.where(
            lane_c == LANE - 1, part(msg_low, 1) + part(msg_low, 2) * part(mine_low, 0), halo_low
        ).astype(BF16)
        halo_high = rcv[t, 1, :, 0:LANE].astype(F32)
        rcv[t, 1, :, 0:LANE] = jnp.where(
            lane_c == 0, part(msg_high, 1) + part(msg_high, 2) * part(mine_high, 0), halo_high
        ).astype(BF16)

        def outer_part(i, carry):
            ws = pl.ds(pl.multiple_of(i * tile, tile), tile)
            out = pl.ds(pl.multiple_of(LANE + i * tile, LANE), tile)
            u[:, out] += (
                times(rcv[t, 0, :, 0:margin], wv[0, ws, 0:margin])
                + times(h[:, LANE:LANE + cut - margin], wv[0, ws, margin:cut])
            ).T
            out = pl.ds(pl.multiple_of(LANE + (subs - 1) * own + i * tile, LANE), tile)
            u[:, out] += (
                times(rcv[t, 1, :, 0:margin], wv[subs - 1, ws, order - margin:order])
                + times(
                    h[:, LANE + rows - (cut - margin):LANE + rows],
                    wv[subs - 1, ws, order - cut:order - margin],
                )
            ).T
            return carry

        lax.fori_loop(0, tiles, outer_part, 0, unroll=True)

    def complete_coarse():
        for copy in neighbour_copies():
            copy.wait()
        lane = lax.broadcasted_iota(jnp.int32, (LANE, LANE), 1)

        def fill(d, carry):
            def block(at):
                return cx[:, pl.ds(pl.multiple_of(at * LANE, LANE), LANE)].astype(F32)

            after = pltpu.roll(block(lax.rem(d + 1, ns)), nm + modes, 1)
            before = pltpu.roll(block(lax.rem(d + ns - 1, ns)), modes, 1)
            both = jnp.where(lane < nm + modes, before, after)
            both = jnp.where(lane < nm, block(d), jnp.where(lane < nm + 2 * modes, both, 0.0))
            cy[:, pl.ds(pl.multiple_of(d * LANE, LANE), LANE)] = both.astype(BF16)
            return carry

        lax.fori_loop(0, ns, fill, 0)

    def coarse_step(t, o):
        for g in range(groups):
            rs = slice(g * group, (g + 1) * group)
            esnd[0, rs, :] = pack([u[rs, LANE + rows - 1:LANE + rows]])
            esnd[1, rs, :] = pack([u[rs, LANE:LANE + 1]])
        rims = rim_copies(o)
        for copy in rims:
            copy.start()

        def coarse_rows(g, carry):
            rs = pl.ds(pl.multiple_of(g * group, group), group)
            for c in range(subs):
                cols = slice(c * own, (c + 1) * own)
                h[rs, LANE + c * own:LANE + (c + 1) * own] = (
                    field[0, rs, cols] - applied(rs, c * own, own)
                ).astype(BF16)
            return carry

        lax.fori_loop(0, groups, coarse_rows, 0)
        to_low = part(rcv[t, 0, :, margin:margin + LANE].astype(F32), 2) * u[:, LANE:LANE + 1]
        h[:, 0:LANE] = jnp.where(lane_c == LANE - 1, to_low, 0.0).astype(BF16)
        to_high = part(rcv[t, 1, :, margin:margin + LANE].astype(F32), 2) * u[:, LANE + rows - 1:LANE + rows]
        h[:, LANE + rows:2 * LANE + rows] = jnp.where(lane_c == 0, to_high, 0.0).astype(BF16)
        projected = dot_nt(h[...], bext[...])
        gbuf[o, :, pl.ds(pl.multiple_of(me * LANE, LANE), LANE)] = projected.astype(BF16)

        def start_gather(k, carry):
            gather_copy(o, k).start()
            return carry

        lax.fori_loop(1, ns, start_gather, 0)
        for copy in rims:
            copy.wait()
        msg = ercv[o, 0].astype(F32)
        u[:, 0:LANE] = jnp.broadcast_to(part(msg, 0), (cases, LANE))
        msg = ercv[o, 1].astype(F32)
        u[:, LANE + rows:2 * LANE + rows] = jnp.broadcast_to(part(msg, 0), (cases, LANE))

        def wait_gather(k, carry):
            gather_wait(o, k).wait()
            return carry

        lax.fori_loop(1, ns, wait_gather, 0)
        coarse = dot_nt(gbuf[o], cy[...]).astype(BF16)
        step = 2 * LANE
        for at in range(0, 2 * LANE + rows, step):
            u[:, at:at + step] += jnp.dot(coarse, bext[:, at:at + step], preferred_element_type=F32)

        def image_rows(g, carry):
            rs = pl.ds(pl.multiple_of(g * group, group), group)
            cross_sum = jnp.zeros((group, LANE), F32)
            square_sum = jnp.zeros((group, LANE), F32)
            for c in range(subs):
                cols = slice(c * own, (c + 1) * own)
                value = applied(rs, c * own, own)
                field[1, rs, cols] = value
                cross = field[0, rs, cols] * value
                square = value * value
                for at in range(0, own, LANE):
                    cross_sum += cross[:, at:at + LANE]
                    square_sum += square[:, at:at + LANE]
            stat[0, rs, :] = cross_sum
            stat[1, rs, :] = square_sum
            return carry

        lax.fori_loop(0, groups, image_rows, 0)
        line = lax.broadcasted_iota(jnp.int32, (8, LANE), 0)
        row_sums = [
            jnp.sum(jnp.where(eye, jnp.sum(stat[at], axis=1, keepdims=True), 0.0), axis=0, keepdims=True)
            for at in range(2)
        ]
        sbuf[o, me] = jnp.where(line == 0, row_sums[0], jnp.where(line == 1, row_sums[1], 0.0))

        def start_sum(k, carry):
            sum_copy(o, k).start()
            return carry

        lax.fori_loop(1, ns, start_sum, 0)

    def get_alpha(o):
        def wait_sum(k, carry):
            sum_wait(o, k).wait()
            return carry

        lax.fori_loop(1, ns, wait_sum, 0)
        totals = jnp.sum(sbuf[o], axis=0)
        alpha_row = totals[0:1] / (totals[1:2] + 1e-06)
        alpha_ref[...] = jnp.broadcast_to(
            jnp.sum(jnp.where(eye, alpha_row, 0.0), axis=1, keepdims=True), (cases, LANE)
        )

    def next_rows(g, carry):
        rs = pl.ds(pl.multiple_of(g * group, group), group)
        alpha = alpha_ref[rs, 0:1]
        for c in range(subs):
            cols = slice(c * own, (c + 1) * own)
            wide = slice(LANE + c * own, LANE + (c + 1) * own)
            sol[rs, cols] += alpha * keep[rs, cols]
            field[0, rs, cols] -= alpha * field[1, rs, cols]
            begun = first[rs, cols] - alpha * u[rs, wide]
            u[rs, wide] = begun
            if OUTER > 2:
                first[rs, cols] = begun
        return carry

    rhs_copy.wait()

    def turn(t, carry):
        o = t // SWEEPS
        begins = lax.rem(t, SWEEPS) == 0
        later = jnp.logical_and(begins, t > 0)
        sweep(t, jnp.where(later, 1, 0))

        @pl.when(t == 0)
        def _():
            first[...] = u[:, LANE:LANE + rows]
            complete_coarse()

        @pl.when(later)
        def _():
            get_alpha(o - 1)
            lax.fori_loop(0, groups, next_rows, 0)

        @pl.when(t == (OUTER - 1) * SWEEPS)
        def _():
            for copy in result_copies[:2]:
                copy.start()

        @pl.when(lax.rem(t, SWEEPS) == SWEEPS - 1)
        def _():
            coarse_step(t, o)

            @pl.when(o < OUTER - 1)
            def _():
                keep[...] = u[:, LANE:LANE + rows]
                u[...] = jnp.zeros_like(u)

        return carry

    lax.fori_loop(0, OUTER * SWEEPS, turn, 0, unroll=False)
    for copy in result_copies[2:]:
        copy.start()
    get_alpha(OUTER - 1)
    for copy in result_copies:
        copy.wait()


def last_kernel(alpha_ref, sol_ref, last_ref, res_ref, img_ref, sol_out, res_out):
    alpha = alpha_ref[:, 0:1]
    sol_out[...] = sol_ref[...] + alpha * last_ref[...]
    res_out[...] = res_ref[...] - alpha * img_ref[...]


def body(right_side, diagonal, coupling, local_inverse, coarse_basis, coarse_inverse):
    ns = lax.axis_size("sector")
    nl = lax.axis_size("lift")
    cases, rows = right_side.shape
    subs, own, order = local_inverse.shape
    modes = coarse_basis.shape[1]
    margin = (order - own) // 2
    steps = SWEEPS * OUTER
    tile = 256
    vmem = pl.BlockSpec(memory_space=pltpu.VMEM)
    hbm = pl.BlockSpec(memory_space=pl.ANY)
    dma = pltpu.SemaphoreType.DMA
    flops = 2 * cases * subs * own * order * steps
    solved, residual, update, image, alpha = pl.pallas_call(
        functools.partial(kernel, ns, nl),
        out_shape=(jax.ShapeDtypeStruct((cases, rows), F32),) * 4
        + (jax.ShapeDtypeStruct((cases, LANE), F32),),
        in_specs=[hbm, vmem, vmem, hbm, vmem, vmem],
        out_specs=(hbm,) * 4 + (vmem,),
        scratch_shapes=[
            pltpu.VMEM((subs, own, order), BF16),
            pltpu.VMEM((cases, rows + 2 * LANE), F32),
            pltpu.VMEM((cases, rows), F32),
            pltpu.VMEM((cases, rows), F32),
            pltpu.VMEM((cases, rows), F32),
            pltpu.VMEM((2, cases, rows), F32),
            pltpu.VMEM((cases, rows + 2 * LANE), BF16),
            pltpu.VMEM((2, cases, margin + LANE), BF16),
            pltpu.VMEM((steps, 2, cases, margin + LANE), BF16),
            pltpu.VMEM((2, cases, LANE), F32),
            pltpu.VMEM((2, cases, LANE), BF16),
            pltpu.VMEM((OUTER, 2, cases, LANE), BF16),
            pltpu.VMEM((LANE, rows + 2 * LANE), BF16),
            pltpu.VMEM((LANE, ns * LANE), BF16),
            pltpu.VMEM((LANE, ns * LANE), BF16),
            pltpu.VMEM((OUTER, cases, ns * LANE), BF16),
            pltpu.VMEM((2, cases, LANE), F32),
            pltpu.VMEM((OUTER, ns, 8, LANE), F32),
            dma, dma((4,)), dma((own // tile,)),
            dma((steps, 2)), dma((steps, 2)),
            dma((OUTER, 2)), dma((OUTER, 2)),
            dma((nl,)), dma((nl,)),
            dma((4,)), dma((4,)),
            dma((OUTER, ns)), dma((OUTER, ns)),
            dma((OUTER, ns)), dma((OUTER, ns)),
        ],
        compiler_params=pltpu.CompilerParams(
            collective_id=0, has_side_effects=True, vmem_limit_bytes=56 * 1024 * 1024
        ),
        cost_estimate=pl.CostEstimate(
            flops=flops, bytes_accessed=2 * subs * own * order, transcendentals=0
        ),
    )(right_side, diagonal[None, :], coupling[None, :], local_inverse, coarse_basis, coarse_inverse)
    group = 16
    wide = pl.BlockSpec((group, rows), lambda i: (i, 0))
    return pl.pallas_call(
        last_kernel,
        grid=(cases // group,),
        out_shape=(jax.ShapeDtypeStruct((cases, rows), F32),) * 2,
        in_specs=[pl.BlockSpec((group, LANE), lambda i: (i, 0))] + [wide] * 4,
        out_specs=(wide, wide),
        compiler_params=pltpu.CompilerParams(vmem_limit_bytes=16 * 1024 * 1024),
    )(alpha, solved, update, residual, image)


def solution(mesh):
    in_specs = (
        P("lift", "sector"),
        P("sector"),
        P("sector"),
        P("sector", None, None),
        P("sector", None, None),
        P("sector", "lift"),
    )
    out_specs = (P("lift", "sector"), P("lift", "sector"))
    return jax.shard_map(body, mesh=mesh, in_specs=in_specs, out_specs=out_specs, check_vma=False)
```

```python
import functools

import jax
import jax.numpy as jnp
from jax import lax
from jax.experimental import pallas as pl
from jax.experimental.pallas import tpu as pltpu
from jax.sharding import PartitionSpec as P

SWEEPS = 4
OUTER = 2
LANE = 128
F32 = jnp.float32
BF16 = jnp.bfloat16
NT = (((1,), (1,)), ((), ()))


def dot_nt(a, b):
    return lax.dot_general(a, b, NT, preferred_element_type=F32)


def times(field, inverse):
    return dot_nt(inverse, field)


def kernel(
    ns, nl,
    rhs_ref, diag_ref, coup_ref, inv_ref, basis_ref, cinv_ref,
    sol_out, res_out, last_out, img_out, alpha_ref,
    wv, u, sol, field, h, far, snd, rcv, edge, esnd, ercv, bext, cx, cy, gbuf, stat, sbuf,
    r_sem, o_sem, w_sem, hs_sem, hr_sem, es_sem, er_sem, ls_sem, lr_sem, ns_sem, nr_sem,
    gs_sem, gr_sem, fs_sem, fr_sem, ss_sem, sr_sem, bs_sem, br_sem,
):
    cases, rows = rhs_ref.shape
    subs, own, order = inv_ref.shape
    margin = (order - own) // 2
    modes = basis_ref.shape[1]
    nm = subs * modes
    tile = wv.shape[1] // w_sem.shape[0]
    tiles = own // tile
    group = 16
    groups = cases // group
    cut = margin + 2 * LANE
    me = lax.axis_index("sector")
    lift = lax.axis_index("lift")
    right = lax.rem(me + 1, ns)
    left = lax.rem(me + ns - 1, ns)

    def w_copy(i):
        return pltpu.make_async_copy(
            inv_ref.at[:, pl.ds(i * tile, tile), :], wv.at[:, pl.ds(i * tile, tile), :], w_sem.at[i]
        )

    rhs_copy = pltpu.make_async_copy(rhs_ref, field.at[0], r_sem)
    rhs_copy.start()
    for i in range(tiles):
        w_copy(i).start()
    result_copies = (
        pltpu.make_async_copy(sol, sol_out, o_sem.at[0]),
        pltpu.make_async_copy(field.at[0], res_out, o_sem.at[1]),
        pltpu.make_async_copy(u.at[:, LANE:LANE + rows], last_out, o_sem.at[2]),
        pltpu.make_async_copy(field.at[1], img_out, o_sem.at[3]),
    )

    def remote(src, dst, send, recv, where):
        return pltpu.make_async_remote_copy(
            src_ref=src, dst_ref=dst, send_sem=send, recv_sem=recv,
            device_id=where, device_id_type=pl.DeviceIdType.MESH,
        )

    bext[...] = jnp.zeros_like(bext)
    for j in range(subs):
        bext[j * modes:(j + 1) * modes, LANE + j * own:LANE + (j + 1) * own] = basis_ref[j]
    cx[...] = jnp.zeros_like(cx)
    half = cinv_ref.shape[1]
    per = half // nm
    lanes = lax.broadcasted_iota(jnp.int32, (nm, LANE), 1)
    for d in range(per):
        start = d * nm
        base = (start // LANE) * LANE
        block = cinv_ref[:, base:base + LANE]
        if start > base:
            block = pltpu.roll(block, LANE - (start - base), 1)
        block = jnp.where(lanes < nm, block, 0.0).astype(BF16)
        cx[0:nm, pl.ds(pl.multiple_of((lift * per + d) * LANE, LANE), LANE)] = block
    barrier = pltpu.get_barrier_semaphore()

    def greet(k, carry):
        pl.semaphore_signal(
            barrier, inc=1, device_id={"sector": lax.rem(me + k, ns)},
            device_id_type=pl.DeviceIdType.MESH,
        )
        return carry

    lax.fori_loop(1, ns, greet, 0)
    for k in range(1, nl):
        pl.semaphore_signal(
            barrier, inc=1, device_id={"lift": lax.rem(lift + k, nl)},
            device_id_type=pl.DeviceIdType.MESH,
        )
    h[...] = jnp.zeros_like(h)
    u[...] = jnp.zeros_like(u)
    sol[...] = jnp.zeros_like(sol)
    pl.semaphore_wait(barrier, ns - 1 + nl - 1)

    def lift_copy(k):
        part = cx.at[0:nm, pl.ds(pl.multiple_of(lift * per * LANE, LANE), per * LANE)]
        return remote(part, part, ls_sem.at[k], lr_sem.at[k], {"lift": lax.rem(lift + k, nl)})

    def lift_wait(k):
        source = lax.rem(lift + nl - k, nl)
        part = cx.at[0:nm, pl.ds(pl.multiple_of(source * per * LANE, LANE), per * LANE)]
        return remote(part, part, ls_sem.at[k], lr_sem.at[k], {"lift": lax.rem(lift + k, nl)})

    def neighbour_copies():
        return (
            remote(cx.at[nm - modes:nm], cx.at[nm:nm + modes], ns_sem.at[0], nr_sem.at[0], {"sector": right}),
            remote(cx.at[0:modes], cx.at[nm + modes:nm + 2 * modes], ns_sem.at[1], nr_sem.at[1], {"sector": left}),
            remote(
                basis_ref.at[subs - 1, :, own - LANE:own], bext.at[nm:nm + modes, 0:LANE],
                ns_sem.at[2], nr_sem.at[2], {"sector": right},
            ),
            remote(
                basis_ref.at[0, :, 0:LANE], bext.at[nm + modes:nm + 2 * modes, LANE + rows:2 * LANE + rows],
                ns_sem.at[3], nr_sem.at[3], {"sector": left},
            ),
        )

    for k in range(1, nl):
        lift_copy(k).start()

    lane_g = lax.broadcasted_iota(jnp.int32, (group, LANE), 1)
    lane_c = lax.broadcasted_iota(jnp.int32, (cases, LANE), 1)
    eye = lax.broadcasted_iota(jnp.int32, (cases, LANE), 0) == lane_c

    def pack(parts):
        out = jnp.zeros((parts[0].shape[0], LANE), F32)
        lane = lane_g
        for at, part in enumerate(parts):
            high = part.astype(BF16).astype(F32)
            out = jnp.where(lane == 2 * at, high, out)
            out = jnp.where(lane == 2 * at + 1, part - high, out)
        return out.astype(BF16)

    def applied(rs, at, width):
        x = u[rs, at:at + width + 2 * LANE]
        span = width + 2 * LANE
        both = pltpu.roll(x, 1, 1)[:, LANE:LANE + width] + pltpu.roll(x, span - 1, 1)[:, LANE:LANE + width]
        cols = slice(at, at + width)
        return diag_ref[:, cols] * x[:, LANE:LANE + width] - coup_ref[:, cols] * both

    def part(msg, at):
        return msg[:, 2 * at:2 * at + 1] + msg[:, 2 * at + 1:2 * at + 2]

    def halo_copies(t):
        return (
            remote(snd.at[0], rcv.at[t, 0], hs_sem.at[t, 0], hr_sem.at[t, 0], {"sector": right}),
            remote(snd.at[1], rcv.at[t, 1], hs_sem.at[t, 1], hr_sem.at[t, 1], {"sector": left}),
        )

    def rim_copies(o):
        return (
            remote(esnd.at[0], ercv.at[o, 0], es_sem.at[o, 0], er_sem.at[o, 0], {"sector": right}),
            remote(esnd.at[1], ercv.at[o, 1], es_sem.at[o, 1], er_sem.at[o, 1], {"sector": left}),
        )

    core = lax.rem(me, 2)
    chip = me // 2
    chips = ns // 2
    sibling = me + 1 - 2 * core

    def block_of(o, source):
        return gbuf.at[o, :, pl.ds(pl.multiple_of(source * LANE, LANE), LANE)]

    def gather_copy(o, k, source):
        target = sibling if isinstance(k, int) else 2 * lax.rem(chip + k, chips) + core
        part = block_of(o, source)
        return remote(part, part, gs_sem.at[o, k], gr_sem.at[o, k], {"sector": target})

    def hand_on(o, k, core_at):
        part = block_of(o, 2 * lax.rem(chip + chips - k, chips) + core_at)
        return remote(part, part, fs_sem.at[o, k], fr_sem.at[o, k], {"sector": sibling})

    def far_copies(at, which):
        return (
            remote(
                field.at[which, :, rows - margin:rows], far.at[at, 0],
                bs_sem.at[at, 0], br_sem.at[at, 0], {"sector": right},
            ),
            remote(
                field.at[which, :, 0:margin], far.at[at, 1],
                bs_sem.at[at, 1], br_sem.at[at, 1], {"sector": left},
            ),
        )

    def sum_copy(o, k):
        return remote(
            sbuf.at[o, me], sbuf.at[o, me], ss_sem.at[o, k], sr_sem.at[o, k],
            {"sector": lax.rem(me + k, ns)},
        )

    def sum_wait(o, k):
        source = lax.rem(me + ns - k, ns)
        return remote(
            sbuf.at[o, source], sbuf.at[o, source], ss_sem.at[o, k], sr_sem.at[o, k],
            {"sector": lax.rem(me + k, ns)},
        )

    def residual_step(t):
        def low_rows(g, carry):
            rs = pl.ds(pl.multiple_of(g * group, group), group)
            hf = field[0, rs, 0:margin] - applied(rs, 0, margin)
            hb = hf.astype(BF16)
            h[rs, LANE:LANE + margin] = hb
            snd[1, rs, 0:margin] = hb
            edge[0, rs, :] = hf[:, 0:LANE]
            snd[1, rs, margin:margin + LANE] = pack(
                [u[rs, LANE:LANE + 1], hf[:, 0:1], jnp.broadcast_to(coup_ref[:, 0:1], (group, 1))]
            )
            hf = field[0, rs, rows - margin:rows] - applied(rs, rows - margin, margin)
            hb = hf.astype(BF16)
            h[rs, LANE + rows - margin:LANE + rows] = hb
            snd[0, rs, 0:margin] = hb
            edge[1, rs, :] = hf[:, margin - LANE:margin]
            snd[0, rs, margin:margin + LANE] = pack(
                [
                    u[rs, LANE + rows - 1:LANE + rows], hf[:, margin - 1:margin],
                    jnp.broadcast_to(coup_ref[:, rows - 1:rows], (group, 1)),
                ]
            )
            return carry

        lax.fori_loop(0, groups, low_rows, 0, unroll=True)
        copies = halo_copies(t)
        for copy in copies:
            copy.start()

        def middle_rows(g, carry):
            rs = pl.ds(pl.multiple_of(g * group, group), group)
            for at in range(margin, rows - margin, own):
                width = min(own, rows - margin - at)
                hf = field[0, rs, at:at + width] - applied(rs, at, width)
                h[rs, LANE + at:LANE + at + width] = hf.astype(BF16)
            return carry

        lax.fori_loop(0, groups, middle_rows, 0)

    def inner_products():
        def inner(i, carry):
            ws = pl.ds(pl.multiple_of(i * tile, tile), tile)
            for j in range(subs):
                low = cut if j == 0 else 0
                high = order - cut if j == subs - 1 else order
                shift = LANE + j * own - margin
                out = pl.ds(pl.multiple_of(LANE + j * own + i * tile, LANE), tile)
                u[:, out] += times(h[:, shift + low:shift + high], wv[j, ws, low:high]).T
            return carry

        lax.fori_loop(0, tiles, inner, 0, unroll=True)

    def take_halos(t):
        for copy in halo_copies(t):
            copy.wait()
        msg_low = rcv[t, 0, :, margin:margin + LANE].astype(F32)
        msg_high = rcv[t, 1, :, margin:margin + LANE].astype(F32)
        mine_low = snd[1, :, margin:margin + LANE].astype(F32)
        mine_high = snd[0, :, margin:margin + LANE].astype(F32)
        tile_low = edge[0]
        h[:, LANE:2 * LANE] = jnp.where(
            lane_c == 0, tile_low + coup_ref[:, 0:LANE] * part(msg_low, 0), tile_low
        ).astype(BF16)
        tile_high = edge[1]
        h[:, rows:LANE + rows] = jnp.where(
            lane_c == LANE - 1, tile_high + coup_ref[:, rows - LANE:rows] * part(msg_high, 0), tile_high
        ).astype(BF16)
        halo_low = rcv[t, 0, :, margin - LANE:margin].astype(F32)
        rcv[t, 0, :, margin - LANE:margin] = jnp.where(
            lane_c == LANE - 1, part(msg_low, 1) + part(msg_low, 2) * part(mine_low, 0), halo_low
        ).astype(BF16)
        halo_high = rcv[t, 1, :, 0:LANE].astype(F32)
        rcv[t, 1, :, 0:LANE] = jnp.where(
            lane_c == 0, part(msg_high, 1) + part(msg_high, 2) * part(mine_high, 0), halo_high
        ).astype(BF16)

    def outer_products(t):
        def outer_part(i, carry):
            ws = pl.ds(pl.multiple_of(i * tile, tile), tile)
            out = pl.ds(pl.multiple_of(LANE + i * tile, LANE), tile)
            u[:, out] += (
                times(rcv[t, 0, :, 0:margin], wv[0, ws, 0:margin])
                + times(h[:, LANE:LANE + cut - margin], wv[0, ws, margin:cut])
            ).T
            out = pl.ds(pl.multiple_of(LANE + (subs - 1) * own + i * tile, LANE), tile)
            u[:, out] += (
                times(rcv[t, 1, :, 0:margin], wv[subs - 1, ws, order - margin:order])
                + times(
                    h[:, LANE + rows - (cut - margin):LANE + rows],
                    wv[subs - 1, ws, order - cut:order - margin],
                )
            ).T
            return carry

        lax.fori_loop(0, tiles, outer_part, 0, unroll=True)

    def complete_coarse():
        for copy in neighbour_copies():
            copy.wait()
        lane = lax.broadcasted_iota(jnp.int32, (LANE, LANE), 1)

        def fill(d, carry):
            def block(at):
                return cx[:, pl.ds(pl.multiple_of(at * LANE, LANE), LANE)].astype(F32)

            after = pltpu.roll(block(lax.rem(d + 1, ns)), nm + modes, 1)
            before = pltpu.roll(block(lax.rem(d + ns - 1, ns)), modes, 1)
            both = jnp.where(lane < nm + modes, before, after)
            both = jnp.where(lane < nm, block(d), jnp.where(lane < nm + 2 * modes, both, 0.0))
            cy[:, pl.ds(pl.multiple_of(d * LANE, LANE), LANE)] = both.astype(BF16)
            return carry

        lax.fori_loop(0, ns, fill, 0)

    def coarse_step(t, o):
        for g in range(groups):
            rs = slice(g * group, (g + 1) * group)
            esnd[0, rs, :] = pack([u[rs, LANE + rows - 1:LANE + rows]])
            esnd[1, rs, :] = pack([u[rs, LANE:LANE + 1]])
        rims = rim_copies(o)
        for copy in rims:
            copy.start()

        def coarse_rows(g, carry):
            rs = pl.ds(pl.multiple_of(g * group, group), group)
            for c in range(subs):
                cols = slice(c * own, (c + 1) * own)
                h[rs, LANE + c * own:LANE + (c + 1) * own] = (
                    field[0, rs, cols] - applied(rs, c * own, own)
                ).astype(BF16)
            return carry

        lax.fori_loop(0, groups, coarse_rows, 0)
        to_low = part(rcv[t, 0, :, margin:margin + LANE].astype(F32), 2) * u[:, LANE:LANE + 1]
        h[:, 0:LANE] = jnp.where(lane_c == LANE - 1, to_low, 0.0).astype(BF16)
        to_high = part(rcv[t, 1, :, margin:margin + LANE].astype(F32), 2) * u[:, LANE + rows - 1:LANE + rows]
        h[:, LANE + rows:2 * LANE + rows] = jnp.where(lane_c == 0, to_high, 0.0).astype(BF16)
        projected = dot_nt(h[...], bext[...])
        gbuf[o, :, pl.ds(pl.multiple_of(me * LANE, LANE), LANE)] = projected.astype(BF16)

        def start_gather(k, carry):
            gather_copy(o, k, me).start()
            return carry

        lax.fori_loop(1, chips, start_gather, 0)
        gather_copy(o, 0, me).start()
        for copy in rims:
            copy.wait()
        msg = ercv[o, 0].astype(F32)
        u[:, 0:LANE] = jnp.broadcast_to(part(msg, 0), (cases, LANE))
        msg = ercv[o, 1].astype(F32)
        u[:, LANE + rows:2 * LANE + rows] = jnp.broadcast_to(part(msg, 0), (cases, LANE))

        def pass_on(k, carry):
            gather_copy(o, k, 2 * lax.rem(chip + chips - k, chips) + core).wait_recv()
            hand_on(o, k, core).start()
            return carry

        lax.fori_loop(1, chips, pass_on, 0)

        def wait_gather(k, carry):
            gather_copy(o, k, me).wait_send()
            hand_on(o, k, core).wait_send()
            hand_on(o, k, 1 - core).wait_recv()
            return carry

        gather_copy(o, 0, me).wait_send()
        gather_copy(o, 0, sibling).wait_recv()
        lax.fori_loop(1, chips, wait_gather, 0)
        coarse = dot_nt(gbuf[o], cy[...]).astype(BF16)
        step = 2 * LANE
        for at in range(0, 2 * LANE + rows, step):
            u[:, at:at + step] += jnp.dot(coarse, bext[:, at:at + step], preferred_element_type=F32)

        def image_rows(g, carry):
            rs = pl.ds(pl.multiple_of(g * group, group), group)
            cross_sum = jnp.zeros((group, LANE), F32)
            square_sum = jnp.zeros((group, LANE), F32)
            for c in range(subs):
                cols = slice(c * own, (c + 1) * own)
                value = applied(rs, c * own, own)
                field[1, rs, cols] = value
                cross = field[0, rs, cols] * value
                square = value * value
                for at in range(0, own, LANE):
                    cross_sum += cross[:, at:at + LANE]
                    square_sum += square[:, at:at + LANE]
            stat[0, rs, :] = cross_sum
            stat[1, rs, :] = square_sum
            return carry

        lax.fori_loop(0, groups, image_rows, 0)
        row_sums = [
            jnp.sum(jnp.where(eye, jnp.sum(stat[at], axis=1, keepdims=True), 0.0), axis=0, keepdims=True)
            for at in range(2)
        ]
        sbuf[o, me] = row_sums[0] + pltpu.roll(row_sums[1], LANE // 2, 1)

        def start_sum(k, carry):
            sum_copy(o, k).start()
            return carry

        lax.fori_loop(1, ns, start_sum, 0)

        @pl.when(o < OUTER - 1)
        def _():
            for copy in far_copies(o + 1, 1):
                copy.start()

    def get_alpha(o):
        def wait_sum(k, carry):
            sum_wait(o, k).wait()
            return carry

        lax.fori_loop(1, ns, wait_sum, 0)
        totals = jnp.sum(sbuf[o], axis=0)
        alpha_row = totals / (pltpu.roll(totals, LANE // 2, 1) + 1e-06)
        alpha_ref[...] = jnp.broadcast_to(
            jnp.sum(jnp.where(eye, alpha_row, 0.0), axis=1, keepdims=True), (cases, LANE)
        )

    def next_rows(g, carry):
        rs = pl.ds(pl.multiple_of(g * group, group), group)
        alpha = alpha_ref[rs, 0:1]
        for c in range(subs):
            cols = slice(c * own, (c + 1) * own)
            wide = slice(LANE + c * own, LANE + (c + 1) * own)
            sol[rs, cols] += alpha * u[rs, wide]
            u[rs, wide] = jnp.zeros((group, own), F32)
            fresh = field[0, rs, cols] - alpha * field[1, rs, cols]
            field[0, rs, cols] = fresh
            h[rs, wide] = fresh.astype(BF16)
        return carry

    rhs_copy.wait()
    for copy in far_copies(0, 0):
        copy.start()
    h[:, LANE:LANE + rows] = field[0].astype(BF16)
    for k in range(1, nl):
        lift_wait(k).wait()
    for copy in neighbour_copies():
        copy.start()
    for i in range(tiles):
        w_copy(i).wait()

    def turn(t, carry):
        o = t // SWEEPS
        begins = lax.rem(t, SWEEPS) == 0

        @pl.when(jnp.logical_and(begins, t > 0))
        def _():
            get_alpha(o - 1)
            lax.fori_loop(0, groups, next_rows, 0)
            u[:, 0:LANE] = jnp.zeros((cases, LANE), F32)
            u[:, LANE + rows:2 * LANE + rows] = jnp.zeros((cases, LANE), F32)
            for copy in far_copies(o, 1):
                copy.wait()
            alpha = alpha_ref[:, 0:1]
            for side in range(2):
                far[0, side] = far[0, side] - alpha * far[o, side]

        @pl.when(t == (OUTER - 1) * SWEEPS)
        def _():
            for copy in result_copies[:2]:
                copy.start()

        @pl.when(jnp.logical_not(begins))
        def _():
            residual_step(t)

        inner_products()

        @pl.when(t == 0)
        def _():
            for copy in far_copies(0, 0):
                copy.wait()

        @pl.when(begins)
        def _():
            for side in range(2):
                rcv[t, side, :, 0:margin] = far[0, side].astype(BF16)

        @pl.when(jnp.logical_not(begins))
        def _():
            take_halos(t)

        outer_products(t)

        @pl.when(t == 0)
        def _():
            complete_coarse()

        @pl.when(lax.rem(t, SWEEPS) == SWEEPS - 1)
        def _():
            coarse_step(t, o)

        return carry

    lax.fori_loop(0, OUTER * SWEEPS, turn, 0, unroll=False)
    for copy in result_copies[2:]:
        copy.start()
    get_alpha(OUTER - 1)
    for copy in result_copies:
        copy.wait()


def last_kernel(alpha_ref, sol_ref, last_ref, res_ref, img_ref, sol_out, res_out):
    alpha = alpha_ref[:, 0:1]
    sol_out[...] = sol_ref[...] + alpha * last_ref[...]
    res_out[...] = res_ref[...] - alpha * img_ref[...]


def body(right_side, diagonal, coupling, local_inverse, coarse_basis, coarse_inverse):
    ns = lax.axis_size("sector")
    nl = lax.axis_size("lift")
    cases, rows = right_side.shape
    subs, own, order = local_inverse.shape
    modes = coarse_basis.shape[1]
    margin = (order - own) // 2
    steps = SWEEPS * OUTER
    tile = 256
    vmem = pl.BlockSpec(memory_space=pltpu.VMEM)
    hbm = pl.BlockSpec(memory_space=pl.ANY)
    dma = pltpu.SemaphoreType.DMA
    flops = 2 * cases * subs * own * order * steps
    solved, residual, update, image, alpha = pl.pallas_call(
        functools.partial(kernel, ns, nl),
        out_shape=(jax.ShapeDtypeStruct((cases, rows), F32),) * 4
        + (jax.ShapeDtypeStruct((cases, LANE), F32),),
        in_specs=[hbm, vmem, vmem, hbm, vmem, vmem],
        out_specs=(hbm,) * 4 + (vmem,),
        scratch_shapes=[
            pltpu.VMEM((subs, own, order), BF16),
            pltpu.VMEM((cases, rows + 2 * LANE), F32),
            pltpu.VMEM((cases, rows), F32),
            pltpu.VMEM((2, cases, rows), F32),
            pltpu.VMEM((cases, rows + 2 * LANE), BF16),
            pltpu.VMEM((OUTER, 2, cases, margin), F32),
            pltpu.VMEM((2, cases, margin + LANE), BF16),
            pltpu.VMEM((steps, 2, cases, margin + LANE), BF16),
            pltpu.VMEM((2, cases, LANE), F32),
            pltpu.VMEM((2, cases, LANE), BF16),
            pltpu.VMEM((OUTER, 2, cases, LANE), BF16),
            pltpu.VMEM((LANE, rows + 2 * LANE), BF16),
            pltpu.VMEM((LANE, ns * LANE), BF16),
            pltpu.VMEM((LANE, ns * LANE), BF16),
            pltpu.VMEM((OUTER, cases, ns * LANE), BF16),
            pltpu.VMEM((2, cases, LANE), F32),
            pltpu.VMEM((OUTER, ns, 1, LANE), F32),
            dma, dma((4,)), dma((own // tile,)),
            dma((steps, 2)), dma((steps, 2)),
            dma((OUTER, 2)), dma((OUTER, 2)),
            dma((nl,)), dma((nl,)),
            dma((4,)), dma((4,)),
            dma((OUTER, ns // 2)), dma((OUTER, ns // 2)),
            dma((OUTER, ns // 2)), dma((OUTER, ns // 2)),
            dma((OUTER, ns)), dma((OUTER, ns)),
            dma((OUTER, 2)), dma((OUTER, 2)),
        ],
        compiler_params=pltpu.CompilerParams(
            collective_id=0, has_side_effects=True, vmem_limit_bytes=56 * 1024 * 1024
        ),
        cost_estimate=pl.CostEstimate(
            flops=flops, bytes_accessed=2 * subs * own * order, transcendentals=0
        ),
    )(right_side, diagonal[None, :], coupling[None, :], local_inverse, coarse_basis, coarse_inverse)
    group = 16
    wide = pl.BlockSpec((group, rows), lambda i: (i, 0))
    return pl.pallas_call(
        last_kernel,
        grid=(cases // group,),
        out_shape=(jax.ShapeDtypeStruct((cases, rows), F32),) * 2,
        in_specs=[pl.BlockSpec((group, LANE), lambda i: (i, 0))] + [wide] * 4,
        out_specs=(wide, wide),
        compiler_params=pltpu.CompilerParams(vmem_limit_bytes=56 * 1024 * 1024),
    )(alpha, solved, update, residual, image)


def solution(mesh):
    in_specs = (
        P("lift", "sector"),
        P("sector"),
        P("sector"),
        P("sector", None, None),
        P("sector", None, None),
        P("sector", "lift"),
    )
    out_specs = (P("lift", "sector"), P("lift", "sector"))
    return jax.shard_map(body, mesh=mesh, in_specs=in_specs, out_specs=out_specs, check_vma=False)
```

```python
import functools

import jax
import jax.numpy as jnp
from jax import lax
from jax.experimental import pallas as pl
from jax.experimental.pallas import tpu as pltpu
from jax.sharding import PartitionSpec as P

SWEEPS = 4
OUTER = 2
LANE = 128
F32 = jnp.float32
BF16 = jnp.bfloat16
NT = (((1,), (1,)), ((), ()))


def dot_nt(a, b):
    return lax.dot_general(a, b, NT, preferred_element_type=F32)


def times(field, inverse):
    return dot_nt(inverse, field)


def kernel(
    ns, nl,
    rhs_ref, diag_ref, coup_ref, inv_ref, basis_ref, cinv_ref,
    sol_out, res_out, last_out, img_out, alpha_ref,
    wv, u, sol, field, h, far, snd, rcv, edge, esnd, ercv, bext, cx, cy, gbuf, stat, sbuf,
    r_sem, o_sem, w_sem, hs_sem, hr_sem, es_sem, er_sem, ls_sem, lr_sem, ns_sem, nr_sem,
    gs_sem, gr_sem, fs_sem, fr_sem, ss_sem, sr_sem, bs_sem, br_sem,
):
    cases, rows = rhs_ref.shape
    subs, own, order = inv_ref.shape
    margin = (order - own) // 2
    modes = basis_ref.shape[1]
    nm = subs * modes
    tiles = w_sem.shape[1]
    tile = own // tiles
    group = 16
    groups = cases // group
    cut = margin + 2 * LANE
    me = lax.axis_index("sector")
    lift = lax.axis_index("lift")
    right = lax.rem(me + 1, ns)
    left = lax.rem(me + ns - 1, ns)

    def w_copy(j, i):
        some = pl.ds(i * tile, tile)
        return pltpu.make_async_copy(inv_ref.at[j, some, :], wv.at[j, some, :], w_sem.at[j, i])

    rhs_copy = pltpu.make_async_copy(rhs_ref, field.at[0], r_sem)
    rhs_copy.start()
    for i in range(tiles):
        for j in range(subs):
            w_copy(j, i).start()
    result_copies = (
        pltpu.make_async_copy(sol, sol_out, o_sem.at[0]),
        pltpu.make_async_copy(field.at[0], res_out, o_sem.at[1]),
        pltpu.make_async_copy(u.at[:, LANE:LANE + rows], last_out, o_sem.at[2]),
        pltpu.make_async_copy(field.at[1], img_out, o_sem.at[3]),
    )

    def remote(src, dst, send, recv, where):
        return pltpu.make_async_remote_copy(
            src_ref=src, dst_ref=dst, send_sem=send, recv_sem=recv,
            device_id=where, device_id_type=pl.DeviceIdType.MESH,
        )

    bext[...] = jnp.zeros_like(bext)
    for j in range(subs):
        bext[j * modes:(j + 1) * modes, LANE + j * own:LANE + (j + 1) * own] = basis_ref[j]
    cx[...] = jnp.zeros_like(cx)
    half = cinv_ref.shape[1]
    per = half // nm
    lanes = lax.broadcasted_iota(jnp.int32, (nm, LANE), 1)
    for d in range(per):
        start = d * nm
        base = (start // LANE) * LANE
        block = cinv_ref[:, base:base + LANE]
        if start > base:
            block = pltpu.roll(block, LANE - (start - base), 1)
        block = jnp.where(lanes < nm, block, 0.0).astype(BF16)
        cx[0:nm, pl.ds(pl.multiple_of((lift * per + d) * LANE, LANE), LANE)] = block
    barrier = pltpu.get_barrier_semaphore()

    def greet(k, carry):
        pl.semaphore_signal(
            barrier, inc=1, device_id={"sector": lax.rem(me + k, ns)},
            device_id_type=pl.DeviceIdType.MESH,
        )
        return carry

    lax.fori_loop(1, ns, greet, 0)
    for k in range(1, nl):
        pl.semaphore_signal(
            barrier, inc=1, device_id={"lift": lax.rem(lift + k, nl)},
            device_id_type=pl.DeviceIdType.MESH,
        )
    h[...] = jnp.zeros_like(h)
    u[...] = jnp.zeros_like(u)
    sol[...] = jnp.zeros_like(sol)
    pl.semaphore_wait(barrier, ns - 1 + nl - 1)

    def lift_copy(k):
        part = cx.at[0:nm, pl.ds(pl.multiple_of(lift * per * LANE, LANE), per * LANE)]
        return remote(part, part, ls_sem.at[k], lr_sem.at[k], {"lift": lax.rem(lift + k, nl)})

    def lift_wait(k):
        source = lax.rem(lift + nl - k, nl)
        part = cx.at[0:nm, pl.ds(pl.multiple_of(source * per * LANE, LANE), per * LANE)]
        return remote(part, part, ls_sem.at[k], lr_sem.at[k], {"lift": lax.rem(lift + k, nl)})

    def neighbour_copies():
        return (
            remote(cx.at[nm - modes:nm], cx.at[nm:nm + modes], ns_sem.at[0], nr_sem.at[0], {"sector": right}),
            remote(cx.at[0:modes], cx.at[nm + modes:nm + 2 * modes], ns_sem.at[1], nr_sem.at[1], {"sector": left}),
            remote(
                basis_ref.at[subs - 1, :, own - LANE:own], bext.at[nm:nm + modes, 0:LANE],
                ns_sem.at[2], nr_sem.at[2], {"sector": right},
            ),
            remote(
                basis_ref.at[0, :, 0:LANE], bext.at[nm + modes:nm + 2 * modes, LANE + rows:2 * LANE + rows],
                ns_sem.at[3], nr_sem.at[3], {"sector": left},
            ),
        )

    for k in range(1, nl):
        lift_copy(k).start()

    lane_g = lax.broadcasted_iota(jnp.int32, (group, LANE), 1)
    lane_c = lax.broadcasted_iota(jnp.int32, (cases, LANE), 1)
    eye = lax.broadcasted_iota(jnp.int32, (cases, LANE), 0) == lane_c

    def pack(parts):
        out = jnp.zeros((parts[0].shape[0], LANE), F32)
        lane = lane_g
        for at, part in enumerate(parts):
            high = part.astype(BF16).astype(F32)
            out = jnp.where(lane == 2 * at, high, out)
            out = jnp.where(lane == 2 * at + 1, part - high, out)
        return out.astype(BF16)

    def applied(rs, at, width):
        x = u[rs, at:at + width + 2 * LANE]
        span = width + 2 * LANE
        both = pltpu.roll(x, 1, 1)[:, LANE:LANE + width] + pltpu.roll(x, span - 1, 1)[:, LANE:LANE + width]
        cols = slice(at, at + width)
        return diag_ref[:, cols] * x[:, LANE:LANE + width] - coup_ref[:, cols] * both

    def part(msg, at):
        return msg[:, 2 * at:2 * at + 1] + msg[:, 2 * at + 1:2 * at + 2]

    def halo_copies(t):
        return (
            remote(snd.at[0], rcv.at[t, 0], hs_sem.at[t, 0], hr_sem.at[t, 0], {"sector": right}),
            remote(snd.at[1], rcv.at[t, 1], hs_sem.at[t, 1], hr_sem.at[t, 1], {"sector": left}),
        )

    def rim_copies(o):
        return (
            remote(esnd.at[0], ercv.at[o, 0], es_sem.at[o, 0], er_sem.at[o, 0], {"sector": right}),
            remote(esnd.at[1], ercv.at[o, 1], es_sem.at[o, 1], er_sem.at[o, 1], {"sector": left}),
        )

    core = lax.rem(me, 2)
    chip = me // 2
    chips = ns // 2
    sibling = me + 1 - 2 * core

    def block_of(o, source):
        return gbuf.at[o, :, pl.ds(pl.multiple_of(source * LANE, LANE), LANE)]

    def gather_copy(o, k, source):
        target = sibling if isinstance(k, int) else 2 * lax.rem(chip + k, chips) + core
        part = block_of(o, source)
        return remote(part, part, gs_sem.at[o, k], gr_sem.at[o, k], {"sector": target})

    def hand_on(o, k, core_at):
        part = block_of(o, 2 * lax.rem(chip + chips - k, chips) + core_at)
        return remote(part, part, fs_sem.at[o, k], fr_sem.at[o, k], {"sector": sibling})

    def far_copies(at, which):
        return (
            remote(
                field.at[which, :, rows - margin:rows], far.at[at, 0],
                bs_sem.at[at, 0], br_sem.at[at, 0], {"sector": right},
            ),
            remote(
                field.at[which, :, 0:margin], far.at[at, 1],
                bs_sem.at[at, 1], br_sem.at[at, 1], {"sector": left},
            ),
        )

    def sum_copy(o, k):
        return remote(
            sbuf.at[o, me], sbuf.at[o, me], ss_sem.at[o, k], sr_sem.at[o, k],
            {"sector": lax.rem(me + k, ns)},
        )

    def sum_wait(o, k):
        source = lax.rem(me + ns - k, ns)
        return remote(
            sbuf.at[o, source], sbuf.at[o, source], ss_sem.at[o, k], sr_sem.at[o, k],
            {"sector": lax.rem(me + k, ns)},
        )

    def residual_step(t):
        def low_rows(g, carry):
            rs = pl.ds(pl.multiple_of(g * group, group), group)
            hf = field[0, rs, 0:margin] - applied(rs, 0, margin)
            hb = hf.astype(BF16)
            h[rs, LANE:LANE + margin] = hb
            snd[1, rs, 0:margin] = hb
            edge[0, rs, :] = hf[:, 0:LANE]
            snd[1, rs, margin:margin + LANE] = pack(
                [u[rs, LANE:LANE + 1], hf[:, 0:1], jnp.broadcast_to(coup_ref[:, 0:1], (group, 1))]
            )
            hf = field[0, rs, rows - margin:rows] - applied(rs, rows - margin, margin)
            hb = hf.astype(BF16)
            h[rs, LANE + rows - margin:LANE + rows] = hb
            snd[0, rs, 0:margin] = hb
            edge[1, rs, :] = hf[:, margin - LANE:margin]
            snd[0, rs, margin:margin + LANE] = pack(
                [
                    u[rs, LANE + rows - 1:LANE + rows], hf[:, margin - 1:margin],
                    jnp.broadcast_to(coup_ref[:, rows - 1:rows], (group, 1)),
                ]
            )
            return carry

        lax.fori_loop(0, groups, low_rows, 0, unroll=True)
        copies = halo_copies(t)
        for copy in copies:
            copy.start()

        def middle_rows(g, carry):
            rs = pl.ds(pl.multiple_of(g * group, group), group)
            for at in range(margin, rows - margin, own):
                width = min(own, rows - margin - at)
                hf = field[0, rs, at:at + width] - applied(rs, at, width)
                h[rs, LANE + at:LANE + at + width] = hf.astype(BF16)
            return carry

        lax.fori_loop(0, groups, middle_rows, 0)

    def inner_products(arriving=False):
        def inner(i, carry):
            ws = pl.ds(i * tile, tile)
            for j in range(subs):
                if arriving:
                    w_copy(j, i).wait()
                low = cut if j == 0 else 0
                high = order - cut if j == subs - 1 else order
                shift = LANE + j * own - margin
                out = pl.ds(LANE + j * own + i * tile, tile)
                u[:, out] += times(h[:, shift + low:shift + high], wv[j, ws, low:high]).T
            return carry

        for i in range(tiles):
            inner(i, 0)

    def take_halos(t):
        for copy in halo_copies(t):
            copy.wait()
        msg_low = rcv[t, 0, :, margin:margin + LANE].astype(F32)
        msg_high = rcv[t, 1, :, margin:margin + LANE].astype(F32)
        mine_low = snd[1, :, margin:margin + LANE].astype(F32)
        mine_high = snd[0, :, margin:margin + LANE].astype(F32)
        tile_low = edge[0]
        h[:, LANE:2 * LANE] = jnp.where(
            lane_c == 0, tile_low + coup_ref[:, 0:LANE] * part(msg_low, 0), tile_low
        ).astype(BF16)
        tile_high = edge[1]
        h[:, rows:LANE + rows] = jnp.where(
            lane_c == LANE - 1, tile_high + coup_ref[:, rows - LANE:rows] * part(msg_high, 0), tile_high
        ).astype(BF16)
        halo_low = rcv[t, 0, :, margin - LANE:margin].astype(F32)
        rcv[t, 0, :, margin - LANE:margin] = jnp.where(
            lane_c == LANE - 1, part(msg_low, 1) + part(msg_low, 2) * part(mine_low, 0), halo_low
        ).astype(BF16)
        halo_high = rcv[t, 1, :, 0:LANE].astype(F32)
        rcv[t, 1, :, 0:LANE] = jnp.where(
            lane_c == 0, part(msg_high, 1) + part(msg_high, 2) * part(mine_high, 0), halo_high
        ).astype(BF16)

    def outer_products(t):
        def outer_part(i, carry):
            ws = pl.ds(pl.multiple_of(i * tile, tile), tile)
            out = pl.ds(pl.multiple_of(LANE + i * tile, LANE), tile)
            u[:, out] += (
                times(rcv[t, 0, :, 0:margin], wv[0, ws, 0:margin])
                + times(h[:, LANE:LANE + cut - margin], wv[0, ws, margin:cut])
            ).T
            out = pl.ds(pl.multiple_of(LANE + (subs - 1) * own + i * tile, LANE), tile)
            u[:, out] += (
                times(rcv[t, 1, :, 0:margin], wv[subs - 1, ws, order - margin:order])
                + times(
                    h[:, LANE + rows - (cut - margin):LANE + rows],
                    wv[subs - 1, ws, order - cut:order - margin],
                )
            ).T
            return carry

        lax.fori_loop(0, tiles, outer_part, 0, unroll=True)

    def complete_coarse():
        for copy in neighbour_copies():
            copy.wait()
        lane = lax.broadcasted_iota(jnp.int32, (LANE, LANE), 1)

        def fill(d, carry):
            def block(at):
                return cx[:, pl.ds(pl.multiple_of(at * LANE, LANE), LANE)].astype(F32)

            after = pltpu.roll(block(lax.rem(d + 1, ns)), nm + modes, 1)
            before = pltpu.roll(block(lax.rem(d + ns - 1, ns)), modes, 1)
            both = jnp.where(lane < nm + modes, before, after)
            both = jnp.where(lane < nm, block(d), jnp.where(lane < nm + 2 * modes, both, 0.0))
            cy[:, pl.ds(pl.multiple_of(d * LANE, LANE), LANE)] = both.astype(BF16)
            return carry

        lax.fori_loop(0, ns, fill, 0)

    def coarse_step(t, o):
        for g in range(groups):
            rs = slice(g * group, (g + 1) * group)
            esnd[0, rs, :] = pack([u[rs, LANE + rows - 1:LANE + rows]])
            esnd[1, rs, :] = pack([u[rs, LANE:LANE + 1]])
        rims = rim_copies(o)
        for copy in rims:
            copy.start()

        def coarse_rows(g, carry):
            rs = pl.ds(pl.multiple_of(g * group, group), group)
            for c in range(subs):
                cols = slice(c * own, (c + 1) * own)
                h[rs, LANE + c * own:LANE + (c + 1) * own] = (
                    field[0, rs, cols] - applied(rs, c * own, own)
                ).astype(BF16)
            return carry

        lax.fori_loop(0, groups, coarse_rows, 0)
        to_low = part(rcv[t, 0, :, margin:margin + LANE].astype(F32), 2) * u[:, LANE:LANE + 1]
        h[:, 0:LANE] = jnp.where(lane_c == LANE - 1, to_low, 0.0).astype(BF16)
        to_high = part(rcv[t, 1, :, margin:margin + LANE].astype(F32), 2) * u[:, LANE + rows - 1:LANE + rows]
        h[:, LANE + rows:2 * LANE + rows] = jnp.where(lane_c == 0, to_high, 0.0).astype(BF16)
        projected = dot_nt(h[...], bext[...])
        gbuf[o, :, pl.ds(pl.multiple_of(me * LANE, LANE), LANE)] = projected.astype(BF16)

        def start_gather(k, carry):
            gather_copy(o, k, me).start()
            return carry

        lax.fori_loop(1, chips, start_gather, 0)
        gather_copy(o, 0, me).start()
        for copy in rims:
            copy.wait()
        msg = ercv[o, 0].astype(F32)
        u[:, 0:LANE] = jnp.broadcast_to(part(msg, 0), (cases, LANE))
        msg = ercv[o, 1].astype(F32)
        u[:, LANE + rows:2 * LANE + rows] = jnp.broadcast_to(part(msg, 0), (cases, LANE))

        def pass_on(k, carry):
            gather_copy(o, k, 2 * lax.rem(chip + chips - k, chips) + core).wait_recv()
            hand_on(o, k, core).start()
            return carry

        lax.fori_loop(1, chips, pass_on, 0)

        def wait_gather(k, carry):
            gather_copy(o, k, me).wait_send()
            hand_on(o, k, core).wait_send()
            hand_on(o, k, 1 - core).wait_recv()
            return carry

        gather_copy(o, 0, me).wait_send()
        gather_copy(o, 0, sibling).wait_recv()
        lax.fori_loop(1, chips, wait_gather, 0)
        coarse = dot_nt(gbuf[o], cy[...]).astype(BF16)
        step = 2 * LANE
        for at in range(0, 2 * LANE + rows, step):
            u[:, at:at + step] += jnp.dot(coarse, bext[:, at:at + step], preferred_element_type=F32)

        def image_rows(g, carry):
            rs = pl.ds(pl.multiple_of(g * group, group), group)
            cross_sum = jnp.zeros((group, LANE), F32)
            square_sum = jnp.zeros((group, LANE), F32)
            for c in range(subs):
                cols = slice(c * own, (c + 1) * own)
                value = applied(rs, c * own, own)
                field[1, rs, cols] = value
                cross = field[0, rs, cols] * value
                square = value * value
                for at in range(0, own, LANE):
                    cross_sum += cross[:, at:at + LANE]
                    square_sum += square[:, at:at + LANE]
            stat[0, rs, :] = cross_sum
            stat[1, rs, :] = square_sum
            return carry

        lax.fori_loop(0, groups, image_rows, 0)
        row_sums = [
            jnp.sum(jnp.where(eye, jnp.sum(stat[at], axis=1, keepdims=True), 0.0), axis=0, keepdims=True)
            for at in range(2)
        ]
        sbuf[o, me] = row_sums[0] + pltpu.roll(row_sums[1], LANE // 2, 1)

        def start_sum(k, carry):
            sum_copy(o, k).start()
            return carry

        lax.fori_loop(1, ns, start_sum, 0)

        @pl.when(o < OUTER - 1)
        def _():
            for copy in far_copies(o + 1, 1):
                copy.start()

    def get_alpha(o):
        def wait_sum(k, carry):
            sum_wait(o, k).wait()
            return carry

        lax.fori_loop(1, ns, wait_sum, 0)
        totals = jnp.sum(sbuf[o], axis=0)
        alpha_row = totals / (pltpu.roll(totals, LANE // 2, 1) + 1e-06)
        alpha_ref[...] = jnp.broadcast_to(
            jnp.sum(jnp.where(eye, alpha_row, 0.0), axis=1, keepdims=True), (cases, LANE)
        )

    def next_rows(g, carry):
        rs = pl.ds(pl.multiple_of(g * group, group), group)
        alpha = alpha_ref[rs, 0:1]
        for c in range(subs):
            cols = slice(c * own, (c + 1) * own)
            wide = slice(LANE + c * own, LANE + (c + 1) * own)
            sol[rs, cols] += alpha * u[rs, wide]
            u[rs, wide] = jnp.zeros((group, own), F32)
            fresh = field[0, rs, cols] - alpha * field[1, rs, cols]
            field[0, rs, cols] = fresh
            h[rs, wide] = fresh.astype(BF16)
        return carry

    rhs_copy.wait()
    for copy in far_copies(0, 0):
        copy.start()
    h[:, LANE:LANE + rows] = field[0].astype(BF16)
    for k in range(1, nl):
        lift_wait(k).wait()
    for copy in neighbour_copies():
        copy.start()
    complete_coarse()
    inner_products(arriving=True)
    for copy in far_copies(0, 0):
        copy.wait()

    def known_halos(t):
        for side in range(2):
            rcv[t, side, :, 0:margin] = far[0, side].astype(BF16)

    known_halos(0)
    outer_products(0)

    def turn(t, carry):
        o = t // SWEEPS
        begins = lax.rem(t, SWEEPS) == 0

        @pl.when(begins)
        def _():
            get_alpha(o - 1)
            lax.fori_loop(0, groups, next_rows, 0)
            u[:, 0:LANE] = jnp.zeros((cases, LANE), F32)
            u[:, LANE + rows:2 * LANE + rows] = jnp.zeros((cases, LANE), F32)
            for copy in far_copies(o, 1):
                copy.wait()
            alpha = alpha_ref[:, 0:1]
            for side in range(2):
                far[0, side] = far[0, side] - alpha * far[o, side]

        @pl.when(t == (OUTER - 1) * SWEEPS)
        def _():
            for copy in result_copies[:2]:
                copy.start()

        @pl.when(jnp.logical_not(begins))
        def _():
            residual_step(t)

        inner_products()

        @pl.when(begins)
        def _():
            known_halos(t)

        @pl.when(jnp.logical_not(begins))
        def _():
            take_halos(t)

        outer_products(t)

        @pl.when(lax.rem(t, SWEEPS) == SWEEPS - 1)
        def _():
            coarse_step(t, o)

        return carry

    lax.fori_loop(1, OUTER * SWEEPS, turn, 0, unroll=False)
    for copy in result_copies[2:]:
        copy.start()
    get_alpha(OUTER - 1)
    for copy in result_copies:
        copy.wait()


def last_kernel(alpha_ref, sol_ref, last_ref, res_ref, img_ref, sol_out, res_out):
    alpha = alpha_ref[:, 0:1]
    sol_out[...] = sol_ref[...] + alpha * last_ref[...]
    res_out[...] = res_ref[...] - alpha * img_ref[...]


def body(right_side, diagonal, coupling, local_inverse, coarse_basis, coarse_inverse):
    ns = lax.axis_size("sector")
    nl = lax.axis_size("lift")
    cases, rows = right_side.shape
    subs, own, order = local_inverse.shape
    modes = coarse_basis.shape[1]
    margin = (order - own) // 2
    steps = SWEEPS * OUTER
    tile = 256
    vmem = pl.BlockSpec(memory_space=pltpu.VMEM)
    hbm = pl.BlockSpec(memory_space=pl.ANY)
    dma = pltpu.SemaphoreType.DMA
    flops = 2 * cases * subs * own * order * steps
    solved, residual, update, image, alpha = pl.pallas_call(
        functools.partial(kernel, ns, nl),
        out_shape=(jax.ShapeDtypeStruct((cases, rows), F32),) * 4
        + (jax.ShapeDtypeStruct((cases, LANE), F32),),
        in_specs=[hbm, vmem, vmem, hbm, vmem, vmem],
        out_specs=(hbm,) * 4 + (vmem,),
        scratch_shapes=[
            pltpu.VMEM((subs, own, order), BF16),
            pltpu.VMEM((cases, rows + 2 * LANE), F32),
            pltpu.VMEM((cases, rows), F32),
            pltpu.VMEM((2, cases, rows), F32),
            pltpu.VMEM((cases, rows + 2 * LANE), BF16),
            pltpu.VMEM((OUTER, 2, cases, margin), F32),
            pltpu.VMEM((2, cases, margin + LANE), BF16),
            pltpu.VMEM((steps, 2, cases, margin + LANE), BF16),
            pltpu.VMEM((2, cases, LANE), F32),
            pltpu.VMEM((2, cases, LANE), BF16),
            pltpu.VMEM((OUTER, 2, cases, LANE), BF16),
            pltpu.VMEM((LANE, rows + 2 * LANE), BF16),
            pltpu.VMEM((LANE, ns * LANE), BF16),
            pltpu.VMEM((LANE, ns * LANE), BF16),
            pltpu.VMEM((OUTER, cases, ns * LANE), BF16),
            pltpu.VMEM((2, cases, LANE), F32),
            pltpu.VMEM((OUTER, ns, 1, LANE), F32),
            dma, dma((4,)), dma((subs, own // tile)),
            dma((steps, 2)), dma((steps, 2)),
            dma((OUTER, 2)), dma((OUTER, 2)),
            dma((nl,)), dma((nl,)),
            dma((4,)), dma((4,)),
            dma((OUTER, ns // 2)), dma((OUTER, ns // 2)),
            dma((OUTER, ns // 2)), dma((OUTER, ns // 2)),
            dma((OUTER, ns)), dma((OUTER, ns)),
            dma((OUTER, 2)), dma((OUTER, 2)),
        ],
        compiler_params=pltpu.CompilerParams(
            collective_id=0, has_side_effects=True, vmem_limit_bytes=46 * 1024 * 1024
        ),
        cost_estimate=pl.CostEstimate(
            flops=flops, bytes_accessed=2 * subs * own * order, transcendentals=0
        ),
    )(right_side, diagonal[None, :], coupling[None, :], local_inverse, coarse_basis, coarse_inverse)
    group = 16
    wide = pl.BlockSpec((group, rows), lambda i: (i, 0))
    return pl.pallas_call(
        last_kernel,
        grid=(cases // group,),
        out_shape=(jax.ShapeDtypeStruct((cases, rows), F32),) * 2,
        in_specs=[pl.BlockSpec((group, LANE), lambda i: (i, 0))] + [wide] * 4,
        out_specs=(wide, wide),
        compiler_params=pltpu.CompilerParams(vmem_limit_bytes=16 * 1024 * 1024),
    )(alpha, solved, update, residual, image)


def solution(mesh):
    in_specs = (
        P("lift", "sector"),
        P("sector"),
        P("sector"),
        P("sector", None, None),
        P("sector", None, None),
        P("sector", "lift"),
    )
    out_specs = (P("lift", "sector"), P("lift", "sector"))
    return jax.shard_map(body, mesh=mesh, in_specs=in_specs, out_specs=out_specs, check_vma=False)
```

```python
import functools

import jax
import jax.numpy as jnp
from jax import lax
from jax.experimental import pallas as pl
from jax.experimental.pallas import tpu as pltpu
from jax.sharding import PartitionSpec as P

SWEEPS = 4
OUTER = 2
LANE = 128
F32 = jnp.float32
BF16 = jnp.bfloat16
NT = (((1,), (1,)), ((), ()))


def dot_nt(a, b):
    return lax.dot_general(a, b, NT, preferred_element_type=F32)


def times(field, inverse):
    return dot_nt(inverse, field)


def kernel(
    ns, nl,
    rhs_ref, diag_ref, coup_ref, inv_ref, basis_ref, cinv_ref,
    sol_out, res_out, last_out, img_out, alpha_ref,
    wv, u, sol, field, h, hold, far, snd, rcv, edge, esnd, ercv, bext, cx, cy, gbuf, stat, sbuf,
    r_sem, o_sem, w_sem, hs_sem, hr_sem, es_sem, er_sem, ls_sem, lr_sem, ns_sem, nr_sem,
    gs_sem, gr_sem, fs_sem, fr_sem, ss_sem, sr_sem, bs_sem, br_sem,
):
    cases, rows = rhs_ref.shape
    subs, own, order = inv_ref.shape
    margin = (order - own) // 2
    modes = basis_ref.shape[1]
    nm = subs * modes
    tile = wv.shape[1] // w_sem.shape[0]
    tiles = own // tile
    group = 16
    groups = cases // group
    cut = margin + 2 * LANE
    me = lax.axis_index("sector")
    lift = lax.axis_index("lift")
    right = lax.rem(me + 1, ns)
    left = lax.rem(me + ns - 1, ns)

    def w_copy(i):
        return pltpu.make_async_copy(
            inv_ref.at[:, pl.ds(i * tile, tile), :], wv.at[:, pl.ds(i * tile, tile), :], w_sem.at[i]
        )

    rhs_copy = pltpu.make_async_copy(rhs_ref, field.at[0], r_sem)
    rhs_copy.start()
    for i in range(tiles):
        w_copy(i).start()
    result_copies = (
        pltpu.make_async_copy(sol, sol_out, o_sem.at[0]),
        pltpu.make_async_copy(field.at[0], res_out, o_sem.at[1]),
        pltpu.make_async_copy(u.at[:, LANE:LANE + rows], last_out, o_sem.at[2]),
        pltpu.make_async_copy(field.at[1], img_out, o_sem.at[3]),
    )

    def remote(src, dst, send, recv, where):
        return pltpu.make_async_remote_copy(
            src_ref=src, dst_ref=dst, send_sem=send, recv_sem=recv,
            device_id=where, device_id_type=pl.DeviceIdType.MESH,
        )

    bext[...] = jnp.zeros_like(bext)
    cx[...] = jnp.zeros_like(cx)
    barrier = pltpu.get_barrier_semaphore()

    def greet(k, carry):
        pl.semaphore_signal(
            barrier, inc=1, device_id={"sector": lax.rem(me + k, ns)},
            device_id_type=pl.DeviceIdType.MESH,
        )
        return carry

    lax.fori_loop(1, ns, greet, 0)
    for k in range(1, nl):
        pl.semaphore_signal(
            barrier, inc=1, device_id={"lift": lax.rem(lift + k, nl)},
            device_id_type=pl.DeviceIdType.MESH,
        )
    for j in range(subs):
        bext[j * modes:(j + 1) * modes, LANE + j * own:LANE + (j + 1) * own] = basis_ref[j]
    half = cinv_ref.shape[1]
    per = half // nm
    lanes = lax.broadcasted_iota(jnp.int32, (nm, LANE), 1)
    for d in range(per):
        start = d * nm
        base = (start // LANE) * LANE
        block = cinv_ref[:, base:base + LANE]
        if start > base:
            block = pltpu.roll(block, LANE - (start - base), 1)
        block = jnp.where(lanes < nm, block, 0.0).astype(BF16)
        cx[0:nm, pl.ds(pl.multiple_of((lift * per + d) * LANE, LANE), LANE)] = block
    h[...] = jnp.zeros_like(h)
    u[...] = jnp.zeros_like(u)
    sol[...] = jnp.zeros_like(sol)
    pl.semaphore_wait(barrier, ns - 1 + nl - 1)

    def lift_copy(k):
        part = cx.at[0:nm, pl.ds(pl.multiple_of(lift * per * LANE, LANE), per * LANE)]
        return remote(part, part, ls_sem.at[k], lr_sem.at[k], {"lift": lax.rem(lift + k, nl)})

    def lift_wait(k):
        source = lax.rem(lift + nl - k, nl)
        part = cx.at[0:nm, pl.ds(pl.multiple_of(source * per * LANE, LANE), per * LANE)]
        return remote(part, part, ls_sem.at[k], lr_sem.at[k], {"lift": lax.rem(lift + k, nl)})

    def neighbour_copies():
        return (
            remote(cx.at[nm - modes:nm], cx.at[nm:nm + modes], ns_sem.at[0], nr_sem.at[0], {"sector": right}),
            remote(cx.at[0:modes], cx.at[nm + modes:nm + 2 * modes], ns_sem.at[1], nr_sem.at[1], {"sector": left}),
            remote(
                basis_ref.at[subs - 1, :, own - LANE:own], bext.at[nm:nm + modes, 0:LANE],
                ns_sem.at[2], nr_sem.at[2], {"sector": right},
            ),
            remote(
                basis_ref.at[0, :, 0:LANE], bext.at[nm + modes:nm + 2 * modes, LANE + rows:2 * LANE + rows],
                ns_sem.at[3], nr_sem.at[3], {"sector": left},
            ),
        )

    for k in range(1, nl):
        lift_copy(k).start()

    lane_g = lax.broadcasted_iota(jnp.int32, (group, LANE), 1)
    lane_c = lax.broadcasted_iota(jnp.int32, (cases, LANE), 1)
    eye = lax.broadcasted_iota(jnp.int32, (cases, LANE), 0) == lane_c

    def pack(parts):
        out = jnp.zeros((parts[0].shape[0], LANE), F32)
        lane = lane_g
        for at, part in enumerate(parts):
            high = part.astype(BF16).astype(F32)
            out = jnp.where(lane == 2 * at, high, out)
            out = jnp.where(lane == 2 * at + 1, part - high, out)
        return out.astype(BF16)

    def applied(rs, at, width):
        x = u[rs, at:at + width + 2 * LANE]
        span = width + 2 * LANE
        both = pltpu.roll(x, 1, 1)[:, LANE:LANE + width] + pltpu.roll(x, span - 1, 1)[:, LANE:LANE + width]
        cols = slice(at, at + width)
        return diag_ref[:, cols] * x[:, LANE:LANE + width] - coup_ref[:, cols] * both

    def part(msg, at):
        return msg[:, 2 * at:2 * at + 1] + msg[:, 2 * at + 1:2 * at + 2]

    def halo_copies(t):
        return (
            remote(snd.at[0], rcv.at[t, 0], hs_sem.at[t, 0], hr_sem.at[t, 0], {"sector": right}),
            remote(snd.at[1], rcv.at[t, 1], hs_sem.at[t, 1], hr_sem.at[t, 1], {"sector": left}),
        )

    def rim_copies(o):
        return (
            remote(esnd.at[0], ercv.at[o, 0], es_sem.at[o, 0], er_sem.at[o, 0], {"sector": right}),
            remote(esnd.at[1], ercv.at[o, 1], es_sem.at[o, 1], er_sem.at[o, 1], {"sector": left}),
        )

    core = lax.rem(me, 2)
    chip = me // 2
    chips = ns // 2
    sibling = me + 1 - 2 * core

    def block_of(o, source):
        return gbuf.at[o, :, pl.ds(pl.multiple_of(source * LANE, LANE), LANE)]

    def gather_copy(o, k, source):
        target = sibling if isinstance(k, int) else 2 * lax.rem(chip + k, chips) + core
        part = block_of(o, source)
        return remote(part, part, gs_sem.at[o, k], gr_sem.at[o, k], {"sector": target})

    def hand_on(o, k, core_at):
        part = block_of(o, 2 * lax.rem(chip + chips - k, chips) + core_at)
        return remote(part, part, fs_sem.at[o, k], fr_sem.at[o, k], {"sector": sibling})

    def far_copies(at, which):
        return (
            remote(
                field.at[which, :, rows - margin:rows], far.at[at, 0],
                bs_sem.at[at, 0], br_sem.at[at, 0], {"sector": right},
            ),
            remote(
                field.at[which, :, 0:margin], far.at[at, 1],
                bs_sem.at[at, 1], br_sem.at[at, 1], {"sector": left},
            ),
        )

    def sum_copy(o, k):
        return remote(
            sbuf.at[o, me], sbuf.at[o, me], ss_sem.at[o, k], sr_sem.at[o, k],
            {"sector": lax.rem(me + k, ns)},
        )

    def sum_wait(o, k):
        source = lax.rem(me + ns - k, ns)
        return remote(
            sbuf.at[o, source], sbuf.at[o, source], ss_sem.at[o, k], sr_sem.at[o, k],
            {"sector": lax.rem(me + k, ns)},
        )

    def residual_step(t):
        def low_rows(g, carry):
            rs = pl.ds(pl.multiple_of(g * group, group), group)
            hf = field[0, rs, 0:margin] - applied(rs, 0, margin)
            hb = hf.astype(BF16)
            h[rs, LANE:LANE + margin] = hb
            snd[1, rs, 0:margin] = hb
            edge[0, rs, :] = hf[:, 0:LANE]
            snd[1, rs, margin:margin + LANE] = pack(
                [u[rs, LANE:LANE + 1], hf[:, 0:1], jnp.broadcast_to(coup_ref[:, 0:1], (group, 1))]
            )
            hf = field[0, rs, rows - margin:rows] - applied(rs, rows - margin, margin)
            hb = hf.astype(BF16)
            h[rs, LANE + rows - margin:LANE + rows] = hb
            snd[0, rs, 0:margin] = hb
            edge[1, rs, :] = hf[:, margin - LANE:margin]
            snd[0, rs, margin:margin + LANE] = pack(
                [
                    u[rs, LANE + rows - 1:LANE + rows], hf[:, margin - 1:margin],
                    jnp.broadcast_to(coup_ref[:, rows - 1:rows], (group, 1)),
                ]
            )
            return carry

        lax.fori_loop(0, groups, low_rows, 0, unroll=True)
        copies = halo_copies(t)
        for copy in copies:
            copy.start()
        outer_products(t - 1, False)

        def middle_rows(g, carry):
            rs = pl.ds(pl.multiple_of(g * group, group), group)
            for at in range(margin, rows - margin, own):
                width = min(own, rows - margin - at)
                hf = field[0, rs, at:at + width] - applied(rs, at, width)
                h[rs, LANE + at:LANE + at + width] = hf.astype(BF16)
            return carry

        lax.fori_loop(0, groups, middle_rows, 0)

    def inner_products():
        def inner(i, carry):
            ws = pl.ds(pl.multiple_of(i * tile, tile), tile)
            for j in range(subs):
                low = cut if j == 0 else 0
                high = order - cut if j == subs - 1 else order
                shift = LANE + j * own - margin
                out = pl.ds(pl.multiple_of(LANE + j * own + i * tile, LANE), tile)
                u[:, out] += times(h[:, shift + low:shift + high], wv[j, ws, low:high]).T
            return carry

        lax.fori_loop(0, tiles, inner, 0, unroll=True)

    def take_halos(t):
        for copy in halo_copies(t):
            copy.wait()
        msg_low = rcv[t, 0, :, margin:margin + LANE].astype(F32)
        msg_high = rcv[t, 1, :, margin:margin + LANE].astype(F32)
        mine_low = snd[1, :, margin:margin + LANE].astype(F32)
        mine_high = snd[0, :, margin:margin + LANE].astype(F32)
        tile_low = edge[0]
        h[:, LANE:2 * LANE] = jnp.where(
            lane_c == 0, tile_low + coup_ref[:, 0:LANE] * part(msg_low, 0), tile_low
        ).astype(BF16)
        tile_high = edge[1]
        h[:, rows:LANE + rows] = jnp.where(
            lane_c == LANE - 1, tile_high + coup_ref[:, rows - LANE:rows] * part(msg_high, 0), tile_high
        ).astype(BF16)
        halo_low = rcv[t, 0, :, margin - LANE:margin].astype(F32)
        rcv[t, 0, :, margin - LANE:margin] = jnp.where(
            lane_c == LANE - 1, part(msg_low, 1) + part(msg_low, 2) * part(mine_low, 0), halo_low
        ).astype(BF16)
        halo_high = rcv[t, 1, :, 0:LANE].astype(F32)
        rcv[t, 1, :, 0:LANE] = jnp.where(
            lane_c == 0, part(msg_high, 1) + part(msg_high, 2) * part(mine_high, 0), halo_high
        ).astype(BF16)

    def keep_rims():
        inside = cut - margin
        hold[0] = h[:, LANE:LANE + inside]
        hold[1] = h[:, LANE + rows - inside:LANE + rows]

    def outer_products(t, near):
        reach = margin + LANE
        spans = (
            ((0, reach), (own - reach, own)) if near else ((reach, own), (0, own - reach))
        )
        low, high = spans
        last = subs - 1
        u[:, LANE + low[0]:LANE + low[1]] += (
            times(rcv[t, 0, :, 0:margin], wv[0, low[0]:low[1], 0:margin])
            + times(hold[0], wv[0, low[0]:low[1], margin:cut])
        ).T
        base = LANE + last * own
        u[:, base + high[0]:base + high[1]] += (
            times(rcv[t, 1, :, 0:margin], wv[last, high[0]:high[1], order - margin:order])
            + times(hold[1], wv[last, high[0]:high[1], order - cut:order - margin])
        ).T

    def complete_coarse():
        for copy in neighbour_copies():
            copy.wait()
        lane = lax.broadcasted_iota(jnp.int32, (LANE, LANE), 1)

        def fill(d, carry):
            def block(at):
                return cx[:, pl.ds(pl.multiple_of(at * LANE, LANE), LANE)].astype(F32)

            after = pltpu.roll(block(lax.rem(d + 1, ns)), nm + modes, 1)
            before = pltpu.roll(block(lax.rem(d + ns - 1, ns)), modes, 1)
            both = jnp.where(lane < nm + modes, before, after)
            both = jnp.where(lane < nm, block(d), jnp.where(lane < nm + 2 * modes, both, 0.0))
            cy[:, pl.ds(pl.multiple_of(d * LANE, LANE), LANE)] = both.astype(BF16)
            return carry

        lax.fori_loop(0, ns, fill, 0)

    def coarse_step(t, o):
        for g in range(groups):
            rs = slice(g * group, (g + 1) * group)
            esnd[0, rs, :] = pack([u[rs, LANE + rows - 1:LANE + rows]])
            esnd[1, rs, :] = pack([u[rs, LANE:LANE + 1]])
        rims = rim_copies(o)
        for copy in rims:
            copy.start()

        def coarse_rows(g, carry):
            rs = pl.ds(pl.multiple_of(g * group, group), group)
            for c in range(subs):
                cols = slice(c * own, (c + 1) * own)
                h[rs, LANE + c * own:LANE + (c + 1) * own] = (
                    field[0, rs, cols] - applied(rs, c * own, own)
                ).astype(BF16)
            return carry

        lax.fori_loop(0, groups, coarse_rows, 0)
        to_low = part(rcv[t, 0, :, margin:margin + LANE].astype(F32), 2) * u[:, LANE:LANE + 1]
        h[:, 0:LANE] = jnp.where(lane_c == LANE - 1, to_low, 0.0).astype(BF16)
        to_high = part(rcv[t, 1, :, margin:margin + LANE].astype(F32), 2) * u[:, LANE + rows - 1:LANE + rows]
        h[:, LANE + rows:2 * LANE + rows] = jnp.where(lane_c == 0, to_high, 0.0).astype(BF16)
        projected = dot_nt(h[...], bext[...])
        gbuf[o, :, pl.ds(pl.multiple_of(me * LANE, LANE), LANE)] = projected.astype(BF16)

        def start_gather(k, carry):
            gather_copy(o, k, me).start()
            return carry

        lax.fori_loop(1, chips, start_gather, 0)
        gather_copy(o, 0, me).start()
        for copy in rims:
            copy.wait()
        msg = ercv[o, 0].astype(F32)
        u[:, 0:LANE] = jnp.broadcast_to(part(msg, 0), (cases, LANE))
        msg = ercv[o, 1].astype(F32)
        u[:, LANE + rows:2 * LANE + rows] = jnp.broadcast_to(part(msg, 0), (cases, LANE))

        def pass_on(k, carry):
            gather_copy(o, k, 2 * lax.rem(chip + chips - k, chips) + core).wait_recv()
            hand_on(o, k, core).start()
            return carry

        lax.fori_loop(1, chips, pass_on, 0)

        def wait_gather(k, carry):
            gather_copy(o, k, me).wait_send()
            hand_on(o, k, core).wait_send()
            hand_on(o, k, 1 - core).wait_recv()
            return carry

        gather_copy(o, 0, me).wait_send()
        gather_copy(o, 0, sibling).wait_recv()
        lax.fori_loop(1, chips, wait_gather, 0)
        coarse = dot_nt(gbuf[o], cy[...]).astype(BF16)
        step = 2 * LANE
        for at in range(0, 2 * LANE + rows, step):
            u[:, at:at + step] += jnp.dot(coarse, bext[:, at:at + step], preferred_element_type=F32)

        def image_rows(g, carry):
            rs = pl.ds(pl.multiple_of(g * group, group), group)
            cross_sum = jnp.zeros((group, LANE), F32)
            square_sum = jnp.zeros((group, LANE), F32)
            for c in range(subs):
                cols = slice(c * own, (c + 1) * own)
                value = applied(rs, c * own, own)
                field[1, rs, cols] = value
                cross = field[0, rs, cols] * value
                square = value * value
                for at in range(0, own, LANE):
                    cross_sum += cross[:, at:at + LANE]
                    square_sum += square[:, at:at + LANE]
            stat[0, rs, :] = cross_sum
            stat[1, rs, :] = square_sum
            return carry

        lax.fori_loop(0, groups, image_rows, 0)
        row_sums = [
            jnp.sum(jnp.where(eye, jnp.sum(stat[at], axis=1, keepdims=True), 0.0), axis=0, keepdims=True)
            for at in range(2)
        ]
        sbuf[o, me] = row_sums[0] + pltpu.roll(row_sums[1], LANE // 2, 1)

        def start_sum(k, carry):
            sum_copy(o, k).start()
            return carry

        lax.fori_loop(1, ns, start_sum, 0)

        @pl.when(o < OUTER - 1)
        def _():
            for copy in far_copies(o + 1, 1):
                copy.start()

    def get_alpha(o):
        def wait_sum(k, carry):
            sum_wait(o, k).wait()
            return carry

        lax.fori_loop(1, ns, wait_sum, 0)
        totals = jnp.sum(sbuf[o], axis=0)
        alpha_row = totals / (pltpu.roll(totals, LANE // 2, 1) + 1e-06)
        alpha_ref[...] = jnp.broadcast_to(
            jnp.sum(jnp.where(eye, alpha_row, 0.0), axis=1, keepdims=True), (cases, LANE)
        )

    def next_rows(g, carry):
        rs = pl.ds(pl.multiple_of(g * group, group), group)
        alpha = alpha_ref[rs, 0:1]
        for c in range(subs):
            cols = slice(c * own, (c + 1) * own)
            wide = slice(LANE + c * own, LANE + (c + 1) * own)
            sol[rs, cols] += alpha * u[rs, wide]
            u[rs, wide] = jnp.zeros((group, own), F32)
            fresh = field[0, rs, cols] - alpha * field[1, rs, cols]
            field[0, rs, cols] = fresh
            h[rs, wide] = fresh.astype(BF16)
        return carry

    rhs_copy.wait()
    for copy in far_copies(0, 0):
        copy.start()
    h[:, LANE:LANE + rows] = field[0].astype(BF16)
    for i in range(tiles):
        w_copy(i).wait()

    def turn(t, carry):
        o = t // SWEEPS
        begins = lax.rem(t, SWEEPS) == 0

        @pl.when(jnp.logical_and(begins, t > 0))
        def _():
            get_alpha(o - 1)
            lax.fori_loop(0, groups, next_rows, 0)
            u[:, 0:LANE] = jnp.zeros((cases, LANE), F32)
            u[:, LANE + rows:2 * LANE + rows] = jnp.zeros((cases, LANE), F32)
            for copy in far_copies(o, 1):
                copy.wait()
            alpha = alpha_ref[:, 0:1]
            for side in range(2):
                far[0, side] = far[0, side] - alpha * far[o, side]

        @pl.when(t == (OUTER - 1) * SWEEPS)
        def _():
            for copy in result_copies[:2]:
                copy.start()

        @pl.when(jnp.logical_not(begins))
        def _():
            residual_step(t)

        inner_products()

        @pl.when(t == 0)
        def _():
            for k in range(1, nl):
                lift_wait(k).wait()
            for copy in neighbour_copies():
                copy.start()
            for copy in far_copies(0, 0):
                copy.wait()

        @pl.when(t == 1)
        def _():
            complete_coarse()

        @pl.when(begins)
        def _():
            for side in range(2):
                rcv[t, side, :, 0:margin] = far[0, side].astype(BF16)

        @pl.when(jnp.logical_not(begins))
        def _():
            take_halos(t)

        keep_rims()
        outer_products(t, True)

        @pl.when(lax.rem(t, SWEEPS) == SWEEPS - 1)
        def _():
            outer_products(t, False)
            coarse_step(t, o)

        return carry

    lax.fori_loop(0, OUTER * SWEEPS, turn, 0, unroll=False)
    for copy in result_copies[2:]:
        copy.start()
    get_alpha(OUTER - 1)
    for copy in result_copies:
        copy.wait()


def last_kernel(alpha_ref, sol_ref, last_ref, res_ref, img_ref, sol_out, res_out):
    alpha = alpha_ref[:, 0:1]
    sol_out[...] = sol_ref[...] + alpha * last_ref[...]
    res_out[...] = res_ref[...] - alpha * img_ref[...]


def body(right_side, diagonal, coupling, local_inverse, coarse_basis, coarse_inverse):
    ns = lax.axis_size("sector")
    nl = lax.axis_size("lift")
    cases, rows = right_side.shape
    subs, own, order = local_inverse.shape
    modes = coarse_basis.shape[1]
    margin = (order - own) // 2
    steps = SWEEPS * OUTER
    tile = 256
    vmem = pl.BlockSpec(memory_space=pltpu.VMEM)
    hbm = pl.BlockSpec(memory_space=pl.ANY)
    dma = pltpu.SemaphoreType.DMA
    flops = 2 * cases * subs * own * order * steps
    solved, residual, update, image, alpha = pl.pallas_call(
        functools.partial(kernel, ns, nl),
        out_shape=(jax.ShapeDtypeStruct((cases, rows), F32),) * 4
        + (jax.ShapeDtypeStruct((cases, LANE), F32),),
        in_specs=[hbm, vmem, vmem, hbm, vmem, vmem],
        out_specs=(hbm,) * 4 + (vmem,),
        scratch_shapes=[
            pltpu.VMEM((subs, own, order), BF16),
            pltpu.VMEM((cases, rows + 2 * LANE), F32),
            pltpu.VMEM((cases, rows), F32),
            pltpu.VMEM((2, cases, rows), F32),
            pltpu.VMEM((cases, rows + 2 * LANE), BF16),
            pltpu.VMEM((2, cases, 2 * LANE), BF16),
            pltpu.VMEM((OUTER, 2, cases, margin), F32),
            pltpu.VMEM((2, cases, margin + LANE), BF16),
            pltpu.VMEM((steps, 2, cases, margin + LANE), BF16),
            pltpu.VMEM((2, cases, LANE), F32),
            pltpu.VMEM((2, cases, LANE), BF16),
            pltpu.VMEM((OUTER, 2, cases, LANE), BF16),
            pltpu.VMEM((LANE, rows + 2 * LANE), BF16),
            pltpu.VMEM((LANE, ns * LANE), BF16),
            pltpu.VMEM((LANE, ns * LANE), BF16),
            pltpu.VMEM((OUTER, cases, ns * LANE), BF16),
            pltpu.VMEM((2, cases, LANE), F32),
            pltpu.VMEM((OUTER, ns, 1, LANE), F32),
            dma, dma((4,)), dma((own // tile,)),
            dma((steps, 2)), dma((steps, 2)),
            dma((OUTER, 2)), dma((OUTER, 2)),
            dma((nl,)), dma((nl,)),
            dma((4,)), dma((4,)),
            dma((OUTER, ns // 2)), dma((OUTER, ns // 2)),
            dma((OUTER, ns // 2)), dma((OUTER, ns // 2)),
            dma((OUTER, ns)), dma((OUTER, ns)),
            dma((OUTER, 2)), dma((OUTER, 2)),
        ],
        compiler_params=pltpu.CompilerParams(
            collective_id=0, has_side_effects=True, vmem_limit_bytes=56 * 1024 * 1024
        ),
        cost_estimate=pl.CostEstimate(
            flops=flops, bytes_accessed=2 * subs * own * order, transcendentals=0
        ),
    )(right_side, diagonal[None, :], coupling[None, :], local_inverse, coarse_basis, coarse_inverse)
    group = 8
    wide = pl.BlockSpec((group, rows), lambda i: (i, 0))
    return pl.pallas_call(
        last_kernel,
        grid=(cases // group,),
        out_shape=(jax.ShapeDtypeStruct((cases, rows), F32),) * 2,
        in_specs=[pl.BlockSpec((group, LANE), lambda i: (i, 0))] + [wide] * 4,
        out_specs=(wide, wide),
        compiler_params=pltpu.CompilerParams(vmem_limit_bytes=56 * 1024 * 1024),
    )(alpha, solved, update, residual, image)


def solution(mesh):
    in_specs = (
        P("lift", "sector"),
        P("sector"),
        P("sector"),
        P("sector", None, None),
        P("sector", None, None),
        P("sector", "lift"),
    )
    out_specs = (P("lift", "sector"), P("lift", "sector"))
    return jax.shard_map(body, mesh=mesh, in_specs=in_specs, out_specs=out_specs, check_vma=False)
```

```python
import functools

import jax
import jax.numpy as jnp
from jax import lax
from jax.experimental import pallas as pl
from jax.experimental.pallas import tpu as pltpu
from jax.sharding import PartitionSpec as P

SWEEPS = 4
OUTER = 2
LANE = 128
F32 = jnp.float32
BF16 = jnp.bfloat16
NT = (((1,), (1,)), ((), ()))


def dot_nt(a, b):
    return lax.dot_general(a, b, NT, preferred_element_type=F32)


def times(field, inverse):
    return dot_nt(inverse, field)


def kernel(
    ns, nl,
    rhs_ref, diag_ref, coup_ref, inv_ref, basis_ref, cinv_ref,
    sol_out, res_out, last_out, img_out, alpha_ref,
    wv, u, sol, field, h, hold, far, snd, rcv, edge, esnd, ercv, bext, cx, cy, gbuf, stat, sbuf,
    r_sem, o_sem, w_sem, hs_sem, hr_sem, es_sem, er_sem, ls_sem, lr_sem, ns_sem, nr_sem,
    gs_sem, gr_sem, fs_sem, fr_sem, ss_sem, sr_sem, bs_sem, br_sem,
):
    cases, rows = rhs_ref.shape
    subs, own, order = inv_ref.shape
    margin = (order - own) // 2
    modes = basis_ref.shape[1]
    nm = subs * modes
    tile = wv.shape[1] // w_sem.shape[0]
    tiles = own // tile
    group = 16
    groups = cases // group
    cut = margin + 2 * LANE
    me = lax.axis_index("sector")
    lift = lax.axis_index("lift")
    right = lax.rem(me + 1, ns)
    left = lax.rem(me + ns - 1, ns)

    def w_copy(i):
        return pltpu.make_async_copy(
            inv_ref.at[:, pl.ds(i * tile, tile), :], wv.at[:, pl.ds(i * tile, tile), :], w_sem.at[i]
        )

    rhs_copy = pltpu.make_async_copy(rhs_ref, field.at[0], r_sem)
    rhs_copy.start()
    for i in range(tiles):
        w_copy(i).start()
    result_copies = (
        pltpu.make_async_copy(sol, sol_out, o_sem.at[0]),
        pltpu.make_async_copy(field.at[0], res_out, o_sem.at[1]),
        pltpu.make_async_copy(u.at[:, LANE:LANE + rows], last_out, o_sem.at[2]),
        pltpu.make_async_copy(field.at[1], img_out, o_sem.at[3]),
    )

    def remote(src, dst, send, recv, where):
        return pltpu.make_async_remote_copy(
            src_ref=src, dst_ref=dst, send_sem=send, recv_sem=recv,
            device_id=where, device_id_type=pl.DeviceIdType.MESH,
        )

    bext[...] = jnp.zeros_like(bext)
    cx[...] = jnp.zeros_like(cx)
    barrier = pltpu.get_barrier_semaphore()

    def greet(k, carry):
        pl.semaphore_signal(
            barrier, inc=1, device_id={"sector": lax.rem(me + k, ns)},
            device_id_type=pl.DeviceIdType.MESH,
        )
        return carry

    lax.fori_loop(1, ns, greet, 0)
    for k in range(1, nl):
        pl.semaphore_signal(
            barrier, inc=1, device_id={"lift": lax.rem(lift + k, nl)},
            device_id_type=pl.DeviceIdType.MESH,
        )
    for j in range(subs):
        bext[j * modes:(j + 1) * modes, LANE + j * own:LANE + (j + 1) * own] = basis_ref[j]
    half = cinv_ref.shape[1]
    per = half // nm
    lanes = lax.broadcasted_iota(jnp.int32, (nm, LANE), 1)
    for d in range(per):
        start = d * nm
        base = (start // LANE) * LANE
        block = cinv_ref[:, base:base + LANE]
        if start > base:
            block = pltpu.roll(block, LANE - (start - base), 1)
        block = jnp.where(lanes < nm, block, 0.0).astype(BF16)
        cx[0:nm, pl.ds(pl.multiple_of((lift * per + d) * LANE, LANE), LANE)] = block
    h[...] = jnp.zeros_like(h)
    u[...] = jnp.zeros_like(u)
    sol[...] = jnp.zeros_like(sol)
    pl.semaphore_wait(barrier, ns - 1 + nl - 1)

    def lift_copy(k):
        part = cx.at[0:nm, pl.ds(pl.multiple_of(lift * per * LANE, LANE), per * LANE)]
        return remote(part, part, ls_sem.at[k], lr_sem.at[k], {"lift": lax.rem(lift + k, nl)})

    def lift_wait(k):
        source = lax.rem(lift + nl - k, nl)
        part = cx.at[0:nm, pl.ds(pl.multiple_of(source * per * LANE, LANE), per * LANE)]
        return remote(part, part, ls_sem.at[k], lr_sem.at[k], {"lift": lax.rem(lift + k, nl)})

    def neighbour_copies():
        return (
            remote(cx.at[nm - modes:nm], cx.at[nm:nm + modes], ns_sem.at[0], nr_sem.at[0], {"sector": right}),
            remote(cx.at[0:modes], cx.at[nm + modes:nm + 2 * modes], ns_sem.at[1], nr_sem.at[1], {"sector": left}),
            remote(
                basis_ref.at[subs - 1, :, own - LANE:own], bext.at[nm:nm + modes, 0:LANE],
                ns_sem.at[2], nr_sem.at[2], {"sector": right},
            ),
            remote(
                basis_ref.at[0, :, 0:LANE], bext.at[nm + modes:nm + 2 * modes, LANE + rows:2 * LANE + rows],
                ns_sem.at[3], nr_sem.at[3], {"sector": left},
            ),
        )

    for k in range(1, nl):
        lift_copy(k).start()

    lane_g = lax.broadcasted_iota(jnp.int32, (group, LANE), 1)
    lane_c = lax.broadcasted_iota(jnp.int32, (cases, LANE), 1)
    eye = lax.broadcasted_iota(jnp.int32, (cases, LANE), 0) == lane_c

    def pack(parts):
        out = jnp.zeros((parts[0].shape[0], LANE), F32)
        lane = lane_g
        for at, part in enumerate(parts):
            high = part.astype(BF16).astype(F32)
            out = jnp.where(lane == 2 * at, high, out)
            out = jnp.where(lane == 2 * at + 1, part - high, out)
        return out.astype(BF16)

    def applied(rs, at, width):
        x = u[rs, at:at + width + 2 * LANE]
        span = width + 2 * LANE
        both = pltpu.roll(x, 1, 1)[:, LANE:LANE + width] + pltpu.roll(x, span - 1, 1)[:, LANE:LANE + width]
        cols = slice(at, at + width)
        return diag_ref[:, cols] * x[:, LANE:LANE + width] - coup_ref[:, cols] * both

    def part(msg, at):
        return msg[:, 2 * at:2 * at + 1] + msg[:, 2 * at + 1:2 * at + 2]

    def halo_copies(t):
        return (
            remote(snd.at[0], rcv.at[t, 0], hs_sem.at[t, 0], hr_sem.at[t, 0], {"sector": right}),
            remote(snd.at[1], rcv.at[t, 1], hs_sem.at[t, 1], hr_sem.at[t, 1], {"sector": left}),
        )

    def rim_copies(o):
        return (
            remote(esnd.at[0], ercv.at[o, 0], es_sem.at[o, 0], er_sem.at[o, 0], {"sector": right}),
            remote(esnd.at[1], ercv.at[o, 1], es_sem.at[o, 1], er_sem.at[o, 1], {"sector": left}),
        )

    core = lax.rem(me, 2)
    chip = me // 2
    chips = ns // 2
    sibling = me + 1 - 2 * core

    def block_of(o, source):
        return gbuf.at[o, :, pl.ds(pl.multiple_of(source * LANE, LANE), LANE)]

    def gather_copy(o, k, source):
        target = sibling if isinstance(k, int) else 2 * lax.rem(chip + k, chips) + core
        part = block_of(o, source)
        return remote(part, part, gs_sem.at[o, k], gr_sem.at[o, k], {"sector": target})

    def hand_on(o, k, core_at):
        part = block_of(o, 2 * lax.rem(chip + chips - k, chips) + core_at)
        return remote(part, part, fs_sem.at[o, k], fr_sem.at[o, k], {"sector": sibling})

    def far_copies(at, which):
        return (
            remote(
                field.at[which, :, rows - margin:rows], far.at[at, 0],
                bs_sem.at[at, 0], br_sem.at[at, 0], {"sector": right},
            ),
            remote(
                field.at[which, :, 0:margin], far.at[at, 1],
                bs_sem.at[at, 1], br_sem.at[at, 1], {"sector": left},
            ),
        )

    def sum_copy(o, k):
        return remote(
            sbuf.at[o, me], sbuf.at[o, me], ss_sem.at[o, k], sr_sem.at[o, k],
            {"sector": lax.rem(me + k, ns)},
        )

    def sum_wait(o, k):
        source = lax.rem(me + ns - k, ns)
        return remote(
            sbuf.at[o, source], sbuf.at[o, source], ss_sem.at[o, k], sr_sem.at[o, k],
            {"sector": lax.rem(me + k, ns)},
        )

    def residual_step(t):
        def low_rows(g, carry):
            rs = pl.ds(pl.multiple_of(g * group, group), group)
            hf = field[0, rs, 0:margin] - applied(rs, 0, margin)
            hb = hf.astype(BF16)
            h[rs, LANE:LANE + margin] = hb
            snd[1, rs, 0:margin] = hb
            edge[0, rs, :] = hf[:, 0:LANE]
            snd[1, rs, margin:margin + LANE] = pack(
                [u[rs, LANE:LANE + 1], hf[:, 0:1], jnp.broadcast_to(coup_ref[:, 0:1], (group, 1))]
            )
            hf = field[0, rs, rows - margin:rows] - applied(rs, rows - margin, margin)
            hb = hf.astype(BF16)
            h[rs, LANE + rows - margin:LANE + rows] = hb
            snd[0, rs, 0:margin] = hb
            edge[1, rs, :] = hf[:, margin - LANE:margin]
            snd[0, rs, margin:margin + LANE] = pack(
                [
                    u[rs, LANE + rows - 1:LANE + rows], hf[:, margin - 1:margin],
                    jnp.broadcast_to(coup_ref[:, rows - 1:rows], (group, 1)),
                ]
            )
            return carry

        lax.fori_loop(0, groups, low_rows, 0, unroll=True)
        copies = halo_copies(t)
        for copy in copies:
            copy.start()
        outer_products(t - 1, False)

        def middle_rows(g, carry):
            rs = pl.ds(pl.multiple_of(g * group, group), group)
            for at in range(margin, rows - margin, own):
                width = min(own, rows - margin - at)
                hf = field[0, rs, at:at + width] - applied(rs, at, width)
                h[rs, LANE + at:LANE + at + width] = hf.astype(BF16)
            return carry

        lax.fori_loop(0, groups, middle_rows, 0)

    def inner_products():
        def inner(i, carry):
            ws = pl.ds(pl.multiple_of(i * tile, tile), tile)
            for j in range(subs):
                low = cut if j == 0 else 0
                high = order - cut if j == subs - 1 else order
                shift = LANE + j * own - margin
                out = pl.ds(pl.multiple_of(LANE + j * own + i * tile, LANE), tile)
                u[:, out] += times(h[:, shift + low:shift + high], wv[j, ws, low:high]).T
            return carry

        lax.fori_loop(0, tiles, inner, 0, unroll=True)

    def take_halos(t):
        for copy in halo_copies(t):
            copy.wait()
        msg_low = rcv[t, 0, :, margin:margin + LANE].astype(F32)
        msg_high = rcv[t, 1, :, margin:margin + LANE].astype(F32)
        mine_low = snd[1, :, margin:margin + LANE].astype(F32)
        mine_high = snd[0, :, margin:margin + LANE].astype(F32)
        tile_low = edge[0]
        h[:, LANE:2 * LANE] = jnp.where(
            lane_c == 0, tile_low + coup_ref[:, 0:LANE] * part(msg_low, 0), tile_low
        ).astype(BF16)
        tile_high = edge[1]
        h[:, rows:LANE + rows] = jnp.where(
            lane_c == LANE - 1, tile_high + coup_ref[:, rows - LANE:rows] * part(msg_high, 0), tile_high
        ).astype(BF16)
        halo_low = rcv[t, 0, :, margin - LANE:margin].astype(F32)
        rcv[t, 0, :, margin - LANE:margin] = jnp.where(
            lane_c == LANE - 1, part(msg_low, 1) + part(msg_low, 2) * part(mine_low, 0), halo_low
        ).astype(BF16)
        halo_high = rcv[t, 1, :, 0:LANE].astype(F32)
        rcv[t, 1, :, 0:LANE] = jnp.where(
            lane_c == 0, part(msg_high, 1) + part(msg_high, 2) * part(mine_high, 0), halo_high
        ).astype(BF16)

    def keep_rims():
        inside = cut - margin
        hold[0] = h[:, LANE:LANE + inside]
        hold[1] = h[:, LANE + rows - inside:LANE + rows]

    def outer_products(t, near):
        reach = margin + LANE
        spans = (
            ((0, reach), (own - reach, own)) if near else ((reach, own), (0, own - reach))
        )
        low, high = spans
        last = subs - 1
        u[:, LANE + low[0]:LANE + low[1]] += (
            times(rcv[t, 0, :, 0:margin], wv[0, low[0]:low[1], 0:margin])
            + times(hold[0], wv[0, low[0]:low[1], margin:cut])
        ).T
        base = LANE + last * own
        u[:, base + high[0]:base + high[1]] += (
            times(rcv[t, 1, :, 0:margin], wv[last, high[0]:high[1], order - margin:order])
            + times(hold[1], wv[last, high[0]:high[1], order - cut:order - margin])
        ).T

    def complete_coarse():
        for copy in neighbour_copies():
            copy.wait()
        lane = lax.broadcasted_iota(jnp.int32, (LANE, LANE), 1)

        def fill(d, carry):
            def block(at):
                return cx[:, pl.ds(pl.multiple_of(at * LANE, LANE), LANE)].astype(F32)

            after = pltpu.roll(block(lax.rem(d + 1, ns)), nm + modes, 1)
            before = pltpu.roll(block(lax.rem(d + ns - 1, ns)), modes, 1)
            both = jnp.where(lane < nm + modes, before, after)
            both = jnp.where(lane < nm, block(d), jnp.where(lane < nm + 2 * modes, both, 0.0))
            cy[:, pl.ds(pl.multiple_of(d * LANE, LANE), LANE)] = both.astype(BF16)
            return carry

        lax.fori_loop(0, ns, fill, 0)

    def coarse_step(t, o):
        for g in range(groups):
            rs = slice(g * group, (g + 1) * group)
            esnd[0, rs, :] = pack([u[rs, LANE + rows - 1:LANE + rows]])
            esnd[1, rs, :] = pack([u[rs, LANE:LANE + 1]])
        rims = rim_copies(o)
        for copy in rims:
            copy.start()

        def coarse_rows(g, carry):
            rs = pl.ds(pl.multiple_of(g * group, group), group)
            for c in range(subs):
                cols = slice(c * own, (c + 1) * own)
                h[rs, LANE + c * own:LANE + (c + 1) * own] = (
                    field[0, rs, cols] - applied(rs, c * own, own)
                ).astype(BF16)
            return carry

        lax.fori_loop(0, groups, coarse_rows, 0)
        to_low = part(rcv[t, 0, :, margin:margin + LANE].astype(F32), 2) * u[:, LANE:LANE + 1]
        h[:, 0:LANE] = jnp.where(lane_c == LANE - 1, to_low, 0.0).astype(BF16)
        to_high = part(rcv[t, 1, :, margin:margin + LANE].astype(F32), 2) * u[:, LANE + rows - 1:LANE + rows]
        h[:, LANE + rows:2 * LANE + rows] = jnp.where(lane_c == 0, to_high, 0.0).astype(BF16)
        projected = dot_nt(h[...], bext[...])
        gbuf[o, :, pl.ds(pl.multiple_of(me * LANE, LANE), LANE)] = projected.astype(BF16)

        def start_gather(k, carry):
            gather_copy(o, k, me).start()
            return carry

        lax.fori_loop(1, chips, start_gather, 0)
        gather_copy(o, 0, me).start()
        for copy in rims:
            copy.wait()
        msg = ercv[o, 0].astype(F32)
        u[:, 0:LANE] = jnp.broadcast_to(part(msg, 0), (cases, LANE))
        msg = ercv[o, 1].astype(F32)
        u[:, LANE + rows:2 * LANE + rows] = jnp.broadcast_to(part(msg, 0), (cases, LANE))

        def pass_on(k, carry):
            gather_copy(o, k, 2 * lax.rem(chip + chips - k, chips) + core).wait_recv()
            hand_on(o, k, core).start()
            return carry

        lax.fori_loop(1, chips, pass_on, 0)

        def wait_gather(k, carry):
            gather_copy(o, k, me).wait_send()
            hand_on(o, k, core).wait_send()
            hand_on(o, k, 1 - core).wait_recv()
            return carry

        gather_copy(o, 0, me).wait_send()
        gather_copy(o, 0, sibling).wait_recv()
        lax.fori_loop(1, chips, wait_gather, 0)
        coarse = dot_nt(gbuf[o], cy[...]).astype(BF16)
        step = 2 * LANE
        for at in range(0, 2 * LANE + rows, step):
            u[:, at:at + step] += jnp.dot(coarse, bext[:, at:at + step], preferred_element_type=F32)

        def image_rows(g, carry):
            rs = pl.ds(pl.multiple_of(g * group, group), group)
            cross_sum = jnp.zeros((group, LANE), F32)
            square_sum = jnp.zeros((group, LANE), F32)
            for c in range(subs):
                cols = slice(c * own, (c + 1) * own)
                value = applied(rs, c * own, own)
                field[1, rs, cols] = value
                cross = field[0, rs, cols] * value
                square = value * value
                for at in range(0, own, LANE):
                    cross_sum += cross[:, at:at + LANE]
                    square_sum += square[:, at:at + LANE]
            stat[0, rs, :] = cross_sum
            stat[1, rs, :] = square_sum
            return carry

        lax.fori_loop(0, groups, image_rows, 0)
        row_sums = [
            jnp.sum(jnp.where(eye, jnp.sum(stat[at], axis=1, keepdims=True), 0.0), axis=0, keepdims=True)
            for at in range(2)
        ]
        sbuf[o, me] = row_sums[0] + pltpu.roll(row_sums[1], LANE // 2, 1)

        def start_sum(k, carry):
            sum_copy(o, k).start()
            return carry

        lax.fori_loop(1, ns, start_sum, 0)

        @pl.when(o < OUTER - 1)
        def _():
            for copy in far_copies(o + 1, 1):
                copy.start()

    def get_alpha(o):
        def wait_sum(k, carry):
            sum_wait(o, k).wait()
            return carry

        lax.fori_loop(1, ns, wait_sum, 0)
        totals = jnp.sum(sbuf[o], axis=0)
        alpha_row = totals / (pltpu.roll(totals, LANE // 2, 1) + 1e-06)
        alpha_ref[...] = jnp.broadcast_to(
            jnp.sum(jnp.where(eye, alpha_row, 0.0), axis=1, keepdims=True), (cases, LANE)
        )

    def next_rows(g, carry):
        rs = pl.ds(pl.multiple_of(g * group, group), group)
        alpha = alpha_ref[rs, 0:1]
        for c in range(subs):
            cols = slice(c * own, (c + 1) * own)
            wide = slice(LANE + c * own, LANE + (c + 1) * own)
            sol[rs, cols] += alpha * u[rs, wide]
            u[rs, wide] = jnp.zeros((group, own), F32)
            fresh = field[0, rs, cols] - alpha * field[1, rs, cols]
            field[0, rs, cols] = fresh
            h[rs, wide] = fresh.astype(BF16)
        return carry

    rhs_copy.wait()
    for copy in far_copies(0, 0):
        copy.start()
    h[:, LANE:LANE + rows] = field[0].astype(BF16)
    for i in range(tiles):
        w_copy(i).wait()

    def turn(t, carry):
        o = t // SWEEPS
        begins = lax.rem(t, SWEEPS) == 0

        @pl.when(jnp.logical_and(begins, t > 0))
        def _():
            get_alpha(o - 1)
            lax.fori_loop(0, groups, next_rows, 0)
            u[:, 0:LANE] = jnp.zeros((cases, LANE), F32)
            u[:, LANE + rows:2 * LANE + rows] = jnp.zeros((cases, LANE), F32)
            for copy in far_copies(o, 1):
                copy.wait()
            alpha = alpha_ref[:, 0:1]
            for side in range(2):
                far[0, side] = far[0, side] - alpha * far[o, side]

        @pl.when(t == (OUTER - 1) * SWEEPS)
        def _():
            for copy in result_copies[:2]:
                copy.start()

        @pl.when(jnp.logical_not(begins))
        def _():
            residual_step(t)

        inner_products()

        @pl.when(t == 0)
        def _():
            for k in range(1, nl):
                lift_wait(k).wait()
            for copy in neighbour_copies():
                copy.start()
            for copy in far_copies(0, 0):
                copy.wait()

        @pl.when(t == 1)
        def _():
            complete_coarse()

        @pl.when(begins)
        def _():
            for side in range(2):
                rcv[t, side, :, 0:margin] = far[0, side].astype(BF16)

        @pl.when(jnp.logical_not(begins))
        def _():
            take_halos(t)

        keep_rims()
        outer_products(t, True)

        @pl.when(lax.rem(t, SWEEPS) == SWEEPS - 1)
        def _():
            outer_products(t, False)
            coarse_step(t, o)

        return carry

    lax.fori_loop(0, OUTER * SWEEPS, turn, 0, unroll=False)
    for copy in result_copies[2:]:
        copy.start()
    get_alpha(OUTER - 1)
    for copy in result_copies:
        copy.wait()


def last_kernel(alpha_ref, sol_ref, last_ref, res_ref, img_ref, sol_out, res_out):
    alpha = alpha_ref[:, 0:1]
    sol_out[...] = sol_ref[...] + alpha * last_ref[...]
    res_out[...] = res_ref[...] - alpha * img_ref[...]


def body(right_side, diagonal, coupling, local_inverse, coarse_basis, coarse_inverse):
    ns = lax.axis_size("sector")
    nl = lax.axis_size("lift")
    cases, rows = right_side.shape
    subs, own, order = local_inverse.shape
    modes = coarse_basis.shape[1]
    margin = (order - own) // 2
    steps = SWEEPS * OUTER
    tile = 256
    vmem = pl.BlockSpec(memory_space=pltpu.VMEM)
    hbm = pl.BlockSpec(memory_space=pl.ANY)
    dma = pltpu.SemaphoreType.DMA
    flops = 2 * cases * subs * own * order * steps
    solved, residual, update, image, alpha = pl.pallas_call(
        functools.partial(kernel, ns, nl),
        out_shape=(jax.ShapeDtypeStruct((cases, rows), F32),) * 4
        + (jax.ShapeDtypeStruct((cases, LANE), F32),),
        in_specs=[hbm, vmem, vmem, hbm, vmem, vmem],
        out_specs=(hbm,) * 4 + (vmem,),
        scratch_shapes=[
            pltpu.VMEM((subs, own, order), BF16),
            pltpu.VMEM((cases, rows + 2 * LANE), F32),
            pltpu.VMEM((cases, rows), F32),
            pltpu.VMEM((2, cases, rows), F32),
            pltpu.VMEM((cases, rows + 2 * LANE), BF16),
            pltpu.VMEM((2, cases, 2 * LANE), BF16),
            pltpu.VMEM((OUTER, 2, cases, margin), F32),
            pltpu.VMEM((2, cases, margin + LANE), BF16),
            pltpu.VMEM((steps, 2, cases, margin + LANE), BF16),
            pltpu.VMEM((2, cases, LANE), F32),
            pltpu.VMEM((2, cases, LANE), BF16),
            pltpu.VMEM((OUTER, 2, cases, LANE), BF16),
            pltpu.VMEM((LANE, rows + 2 * LANE), BF16),
            pltpu.VMEM((LANE, ns * LANE), BF16),
            pltpu.VMEM((LANE, ns * LANE), BF16),
            pltpu.VMEM((OUTER, cases, ns * LANE), BF16),
            pltpu.VMEM((2, cases, LANE), F32),
            pltpu.VMEM((OUTER, ns, 1, LANE), F32),
            dma, dma((4,)), dma((own // tile,)),
            dma((steps, 2)), dma((steps, 2)),
            dma((OUTER, 2)), dma((OUTER, 2)),
            dma((nl,)), dma((nl,)),
            dma((4,)), dma((4,)),
            dma((OUTER, ns // 2)), dma((OUTER, ns // 2)),
            dma((OUTER, ns // 2)), dma((OUTER, ns // 2)),
            dma((OUTER, ns)), dma((OUTER, ns)),
            dma((OUTER, 2)), dma((OUTER, 2)),
        ],
        compiler_params=pltpu.CompilerParams(
            collective_id=0, has_side_effects=True, vmem_limit_bytes=56 * 1024 * 1024
        ),
        cost_estimate=pl.CostEstimate(
            flops=flops, bytes_accessed=2 * subs * own * order, transcendentals=0
        ),
    )(right_side, diagonal[None, :], coupling[None, :], local_inverse, coarse_basis, coarse_inverse)
    group = 32
    wide = pl.BlockSpec((group, rows), lambda i: (i, 0))
    return pl.pallas_call(
        last_kernel,
        grid=(cases // group,),
        out_shape=(jax.ShapeDtypeStruct((cases, rows), F32),) * 2,
        in_specs=[pl.BlockSpec((group, LANE), lambda i: (i, 0))] + [wide] * 4,
        out_specs=(wide, wide),
        compiler_params=pltpu.CompilerParams(vmem_limit_bytes=56 * 1024 * 1024),
    )(alpha, solved, update, residual, image)


def solution(mesh):
    in_specs = (
        P("lift", "sector"),
        P("sector"),
        P("sector"),
        P("sector", None, None),
        P("sector", None, None),
        P("sector", "lift"),
    )
    out_specs = (P("lift", "sector"), P("lift", "sector"))
    return jax.shard_map(body, mesh=mesh, in_specs=in_specs, out_specs=out_specs, check_vma=False)
```
